256 devices in a mesh: adapter: 8 (over z), tensor: 32 (over y, x, core).
Axes of the slice: x: 4, y: 4, z: 8, core: 2. Of those that a mesh axis runs over, the one named last changes fastest.
Arguments:
- hidden_rows: bfloat16 [6144, 8192], P('adapter', 'tensor'), may hold values from -6 to 6
- query_weight: bfloat16 [8192, 8192], P(None, 'tensor'), may hold values from -0.0625 to 0.0625
- down_panels: bfloat16 [192, 64, 8192], P('adapter', None, 'tensor'), may hold values from -0.0625 to 0.0625
- up_panels: bfloat16 [192, 64, 8192], P('adapter', None, 'tensor'), may hold values from -0.75 to 0.75
- store_index: int32 [192], replicated, may hold values from 0 to 191, each once
- requests: int32 [8, 8], replicated, may hold values from 0 to 191, as said below
- row_slot: int32 [6144], P('adapter'), may hold values from 0 to 7
Outputs:
- query_out: bfloat16 [6144, 8192], P('adapter', 'tensor')
The draws below stay inside these ranges and needn't reach their ends.
Inputs may be any that keep to these rules, and one draw needn't show every extreme that they name: `requests`: the 8 ids of each group are distinct adapter ids. `store_index`: each adapter id has its own storage slot.
All inputs are finite; a program needn't handle non-finite values.
Results may differ from the reference program's by a relative error of at most 0.003.
Values may be sent and summed in bfloat16 or wider, within the bound.
No kernel may reach another device: no remote copies, remote signals or barrier semaphores. Data moves between devices by JAX's collectives and lax.ppermute only.
A program may use at most 128 MiB of HBM per device.

```python
import math
import jax
import jax.numpy as jnp
import numpy as np
from jax import lax

D = 8192
ADAPTER_RANK = 64
ROWS_PER_INDEX = 768
GROUP_REQUESTS = 8
ROWS = 6144
ADAPTERS = 192
N_ADAPTER = 8


def draw_requests(key, part):
    key = jax.random.fold_in(key, 7)
    keys = jax.random.split(key, N_ADAPTER)
    return jax.vmap(lambda each: jax.random.permutation(each, ADAPTERS)[:GROUP_REQUESTS])(keys).astype(jnp.int32)


def plant(result, rng, smallest, largest):
    index_at = [jax.random.randint(jax.random.fold_in(rng, axis), (), 0, length) for axis, length in enumerate(result.shape)]
    main_axis = result.shape.index(max(result.shape))
    next_to = index_at[:main_axis] + [(index_at[main_axis] + 1) % result.shape[main_axis]] + index_at[main_axis + 1:]
    return result.at[tuple(index_at)].set(smallest).at[tuple(next_to)].set(largest)


def levels(rng, extent, pieces, least, largest):
    level, own = 1.0, jax.random.fold_in(rng, 6)
    for position, parts in pieces:
        heights = jnp.exp(jax.random.uniform(jax.random.fold_in(own, position), (parts,), jnp.float32, least / len(pieces), largest / len(pieces)))
        level = level * jnp.repeat(heights, extent[position] // parts).reshape([-1 if axis == position else 1 for axis in range(len(extent))])
    return level


def rank_bounds(amount, lean):
    weights = [(1 << 20) // math.isqrt(rank ** lean) + 1 for rank in range(1, amount + 1)]
    width = 1 + sum(weights) // (1 << 30)
    return np.cumsum(np.array([max(1, weight // width) for weight in weights]))


def ranked(rng, shape, count, lean):
    table = rank_bounds(count, lean)
    lot = jax.random.randint(jax.random.fold_in(rng, 1), shape, 0, int(table[count - 1]))
    standing = jnp.searchsorted(jnp.asarray(table, jnp.int32), lot, side="right")
    return jax.random.permutation(jax.random.fold_in(rng, 2), count)[standing].astype(jnp.int32)


def noise(key, dims, width, most, pieces=(), kind=jnp.bfloat16):
    array = jax.random.normal(key, dims, jnp.float32) * width
    if len(pieces) > 0:
        array = levels(key, dims, pieces, -0.22, 0.18) * array
    return jnp.clip(array, min=-most, max=most).astype(kind)


def setup_inputs(seed: int = 0) -> dict:
    key_of = jax.random.split(jax.random.key(seed), 8)
    return {
        "hidden_rows": noise(key_of[0], (ROWS, D), 1.0, 6.0, ((0, 8), (1, 32))),
        "query_weight": noise(key_of[1], (D, D), D ** -0.5, 0.0625, ((1, 32),)),
        "down_panels": noise(key_of[2], (ADAPTERS, ADAPTER_RANK, D), D ** -0.5, 0.0625, ((0, 8), (2, 32))),
        "up_panels": noise(key_of[3], (ADAPTERS, ADAPTER_RANK, D), ADAPTER_RANK ** -0.5, 0.75, ((0, 8), (2, 32))),
        "store_index": jax.random.permutation(key_of[4], ADAPTERS).astype(jnp.int32),
        "requests": draw_requests(jax.random.fold_in(key_of[7], 71), 0),
        "row_slot": plant(ranked(key_of[6], (ROWS,), GROUP_REQUESTS, 2), jax.random.fold_in(key_of[6], 3), 0, GROUP_REQUESTS - 1).astype(jnp.int32),
    }


adapter_scale = 0.5


def reference(hidden_rows, query_weight, down_panels, up_panels, store_index, requests, row_slot):
    base_query = jnp.dot(hidden_rows, query_weight, preferred_element_type=jnp.float32)
    output_rows = []
    for row_group in range(N_ADAPTER):
        rows_here = hidden_rows[row_group * ROWS_PER_INDEX:(row_group + 1) * ROWS_PER_INDEX]
        slots_here = row_slot[row_group * ROWS_PER_INDEX:(row_group + 1) * ROWS_PER_INDEX]
        storage = store_index[requests[row_group]]
        down_flat = down_panels[storage].reshape(GROUP_REQUESTS * ADAPTER_RANK, D)
        flat_up_weight = up_panels[storage].reshape(GROUP_REQUESTS * ADAPTER_RANK, D)
        down_projected = lax.dot_general(rows_here, down_flat, (((1,), (1,)), ((), ())), preferred_element_type=jnp.float32)
        selection_mask = (slots_here[:, None] == jnp.arange(GROUP_REQUESTS, dtype=jnp.int32)[None, :]).astype(jnp.float32)
        scaled_delta = (down_projected.reshape(ROWS_PER_INDEX, GROUP_REQUESTS, ADAPTER_RANK) * selection_mask[:, :, None] * adapter_scale).reshape(ROWS_PER_INDEX, GROUP_REQUESTS * ADAPTER_RANK)
        scaled_delta = scaled_delta.astype(jnp.bfloat16)
        adapter_delta = jnp.dot(scaled_delta, flat_up_weight, preferred_element_type=jnp.float32)
        output_rows.append(base_query[row_group * ROWS_PER_INDEX:(row_group + 1) * ROWS_PER_INDEX] + adapter_delta)
    return jnp.concatenate(output_rows, axis=0).astype(jnp.bfloat16)
```

```python
import functools

import jax
import jax.numpy as jnp
from jax import lax
from jax.experimental import pallas as pl
from jax.experimental.pallas import tpu as pltpu
from jax.sharding import PartitionSpec as P

adapter_scale = 0.5
f32, bf16 = jnp.float32, jnp.bfloat16
NZ, NY, NX, NC = 8, 4, 4, 2
ANY = pl.BlockSpec(memory_space=pl.ANY)
SMEM = pl.BlockSpec(memory_space=pltpu.SMEM)
VMEM = pl.BlockSpec(memory_space=pltpu.VMEM)


def send(value, to):
    pairs = []
    for z in range(NZ):
        for y in range(NY):
            for x in range(NX):
                for c in range(NC):
                    tz, ty, tx, tc = to(z, y, x, c)
                    here = ((z * NY + y) * NX + x) * NC + c
                    there = ((tz % NZ * NY + ty % NY) * NX + tx % NX) * NC + tc
                    pairs.append((here, there))
    return lax.ppermute(value, ("adapter", "tensor"), pairs)


def to_sibling(value):
    return send(value, lambda z, y, x, c: (z, y, x, 1 - c))


def along_z(value):
    return send(value, lambda z, y, x, c: (z + 1 - 2 * c, y, x, c))


def along_x(value, step):
    return send(value, lambda z, y, x, c: (z, y, x + step, c))


def along_y(value, step):
    return send(value, lambda z, y, x, c: (z, y + step, x, c))


def fill_kernel(local_ref, base_ref, mine_ref, sib_ref, out_ref, sems):
    def copies(j):
        k = local_ref[j]
        return (
            pltpu.make_async_copy(mine_ref.at[k], out_ref.at[0, j], sems.at[0, j]),
            pltpu.make_async_copy(sib_ref.at[k], out_ref.at[1, j], sems.at[1, j]),
        )

    count = out_ref.shape[1]
    for j in range(count):
        @pl.when(local_ref[j] >= 0)
        def _():
            for copy in copies(j):
                copy.start()
    for j in range(count):
        @pl.when(local_ref[j] >= 0)
        def _():
            for copy in copies(j):
                copy.wait()


def fill(base, mine, sib, local):
    return pl.pallas_call(
        fill_kernel,
        out_shape=jax.ShapeDtypeStruct(base.shape, base.dtype),
        in_specs=[SMEM, ANY, ANY, ANY],
        out_specs=ANY,
        input_output_aliases={1: 0},
        scratch_shapes=[pltpu.SemaphoreType.DMA((2, base.shape[1]))],
    )(local, base, mine, sib)


def shrink_kernel(pick_ref, plus_ref, minus_ref, own_ref, hidden_ref, slot_ref, out_ref):
    total = jnp.zeros(out_ref.shape, f32)
    hidden = hidden_ref[...]
    slot = slot_ref[...]
    for j in range(plus_ref.shape[0]):
        kind = pick_ref[j]
        panel = jnp.where(kind == 1, plus_ref[j], jnp.where(kind == 2, minus_ref[j], own_ref[j]))
        part = lax.dot_general(panel, hidden, (((1,), (1,)), ((), ())), preferred_element_type=f32)
        total = jnp.where(slot == j, part, total)
    out_ref[...] = total


def expand_kernel(pick_ref, plus_ref, minus_ref, own_ref, scaled_ref, slot_ref, base_ref, out_ref):
    scaled = scaled_ref[...]
    slot = slot_ref[...]
    zero = jnp.zeros(scaled.shape, scaled.dtype)
    total = base_ref[...]
    for j in range(plus_ref.shape[0]):
        kind = pick_ref[j]
        panel = jnp.where(kind == 1, plus_ref[j], jnp.where(kind == 2, minus_ref[j], own_ref[j]))
        mine = jnp.where(slot == j, scaled, zero)
        total += lax.dot_general(mine, panel, (((0,), (0,)), ((), ())), preferred_element_type=f32)
    out_ref[...] = total.astype(out_ref.dtype)


def per_device(hidden_rows, query_weight, down_panels, up_panels, store_index, requests, row_slot):
    rows, feats = hidden_rows.shape
    stored, rank, columns = down_panels.shape
    wanted = requests.shape[1]
    half = wanted // 2
    z = lax.axis_index("adapter")
    c = lax.axis_index("tensor") % 2
    sign = 1 - 2 * c

    with jax.named_scope("hidden_gather"):
        hidden_all = lax.all_gather(hidden_rows, "tensor", axis=1, tiled=True)

    groups = (z + sign * jnp.arange(5, dtype=jnp.int32)) % NZ
    onehot = (requests[groups][:, :, None] == jnp.arange(store_index.shape[0], dtype=jnp.int32)).astype(jnp.int32)
    slots = jnp.sum(onehot * store_index[None, None, :], axis=2)
    local = slots - z * stored
    local = jnp.where((local >= 0) & (local < stored), local, -1)
    far = lax.dynamic_slice_in_dim(local[4], half * c, half)
    behind = (z - slots[0] // stored) % NZ
    from_below = (behind < 4) | ((behind == 4) & (jnp.arange(wanted) < half))
    pick = jnp.where(behind == 0, 0, jnp.where(from_below, 1, 2)).astype(jnp.int32)

    def collect(panels):
        sib = to_sibling(panels)
        going = fill(jnp.zeros((2, half, rank, columns), bf16), panels, sib, far)
        going = along_z(going)
        empty = jnp.zeros_like(going)
        going = jnp.concatenate(
            (jnp.where(c == 0, going, empty), jnp.where(c == 0, empty, going)), axis=1
        )
        for distance in (3, 2, 1):
            going = along_z(fill(going, panels, sib, local[distance]))
        other = to_sibling(going[1])
        plus = jnp.where(c == 0, going[0], other)
        minus = jnp.where(c == 0, other, going[0])
        return plus, minus

    def own(panels):
        at = jnp.maximum(local[0], 0)
        return jnp.stack([lax.dynamic_index_in_dim(panels, at[j], 0, keepdims=False) for j in range(wanted)])

    with jax.named_scope("down_fetch"):
        down_plus, down_minus = collect(down_panels)
        down_own = own(down_panels)
    with jax.named_scope("up_fetch"):
        up_plus, up_minus = collect(up_panels)
        up_own = own(up_panels)

    slot_row = row_slot.reshape(1, rows)
    with jax.named_scope("shrink"):
        part = pl.pallas_call(
            shrink_kernel,
            out_shape=jax.ShapeDtypeStruct((rank, rows), f32),
            in_specs=[SMEM] + [VMEM] * 5,
            out_specs=VMEM,
        )(pick, down_plus, down_minus, down_own, hidden_rows, slot_row)
    with jax.named_scope("shrink_sum"):
        left, right = part[:, : rows // 2], part[:, rows // 2 :]
        part = jnp.where(c == 0, left, right) + to_sibling(jnp.where(c == 0, right, left))
        part = part + along_x(part, 1) + along_x(part, -1) + along_x(part, 2)
        part = part + along_y(part, 1) + along_y(part, -1) + along_y(part, 2)
        scaled = (part * adapter_scale).astype(bf16)
        other = to_sibling(scaled)
        scaled = jnp.concatenate((jnp.where(c == 0, scaled, other), jnp.where(c == 0, other, scaled)), axis=1)
    with jax.named_scope("base"):
        base = jnp.dot(hidden_all, query_weight, preferred_element_type=f32)
    with jax.named_scope("expand"):
        return pl.pallas_call(
            expand_kernel,
            out_shape=jax.ShapeDtypeStruct((rows, columns), bf16),
            in_specs=[SMEM] + [VMEM] * 6,
            out_specs=VMEM,
        )(pick, up_plus, up_minus, up_own, scaled, slot_row, base)


def solution(mesh):
    return jax.shard_map(
        per_device,
        mesh=mesh,
        in_specs=(
            P("adapter", "tensor"),
            P(None, "tensor"),
            P("adapter", None, "tensor"),
            P("adapter", None, "tensor"),
            P(),
            P(),
            P("adapter"),
        ),
        out_specs=P("adapter", "tensor"),
        check_vma=False,
    )
```

```python
import jax
import jax.numpy as jnp
from jax import lax
from jax.experimental import pallas as pl
from jax.experimental.pallas import tpu as pltpu
from jax.sharding import PartitionSpec as P

adapter_scale = 0.5
f32, bf16, i32 = jnp.float32, jnp.bfloat16, jnp.int32
NZ, NY, NX, NC = 8, 4, 4, 2
WANTED = 8
INDEX = NZ * WANTED
SMEM = pl.BlockSpec(memory_space=pltpu.SMEM)
VMEM = pl.BlockSpec(memory_space=pltpu.VMEM)
HBM = pl.BlockSpec(memory_space=pltpu.HBM)
ANY = pl.BlockSpec(memory_space=pl.ANY)
LIMIT = pltpu.CompilerParams(vmem_limit_bytes=48 * 1024 * 1024)


def kernel_call(kernel, out_shape, *operands, scratch=(), specs=None, out=VMEM):
    return pl.pallas_call(
        kernel,
        out_shape=out_shape,
        in_specs=[spec if spec else SMEM if v.dtype == i32 and v.size <= 256 else VMEM for v, spec in zip(operands, specs or [None] * len(operands))],
        out_specs=jax.tree.map(lambda _: out, out_shape),
        scratch_shapes=list(scratch),
        compiler_params=LIMIT,
    )(*operands)


def send(value, to):
    pairs = []
    for z in range(NZ):
        for y in range(NY):
            for x in range(NX):
                for c in range(NC):
                    tz, ty, tx, tc = to(z, y, x, c)
                    here = ((z * NY + y) * NX + x) * NC + c
                    there = ((tz % NZ * NY + ty % NY) * NX + tx % NX) * NC + tc
                    pairs.append((here, there))
    return lax.ppermute(value, ("adapter", "tensor"), pairs)


def to_sibling(value):
    return send(value, lambda z, y, x, c: (z, y, x, 1 - c))


def along_z(value, cross=0):
    return send(value, lambda z, y, x, c: (z + 1 - 2 * c, y, x, c ^ cross))


def along_x(value, step):
    return send(value, lambda z, y, x, c: (z, y, x + step, c))


def along_y(value, step):
    return send(value, lambda z, y, x, c: (z, y + step, x, c))


def along_first(value, step):
    return send(value, lambda z, y, x, c: (z, y + step * c, x + step * (1 - c), c))


def along_second(value, step):
    return send(value, lambda z, y, x, c: (z, y + step * (1 - c), x + step * c, c))


def spread_kernel(table_ref, down_ref, up_ref, out_ref):
    stored = down_ref.shape[0]

    def slot(i, carry):
        local = table_ref[INDEX + table_ref[i]] - lax.axis_index("adapter") * stored
        at, here = jnp.clip(local, 0, stored - 1), (local >= 0) & (local < stored)
        for kind, store in enumerate((down_ref, up_ref)):
            panel = store[at]
            out_ref[i, kind] = jnp.where(here, panel, jnp.zeros_like(panel))
        return carry

    lax.fori_loop(0, out_ref.shape[0], slot, 0, unroll=4)


def shrink_kernel(panels_ref, hidden_ref, slot_ref, keep_ref, give_ref):
    wanted, _, rank, _ = panels_ref.shape
    rows = hidden_ref.shape[0]
    core = lax.rem(lax.axis_index("tensor"), 2)

    def one(j, total):
        part = lax.dot_general(
            panels_ref[j, 0], hidden_ref[...], (((1,), (1,)), ((), ())), preferred_element_type=f32
        )
        return jnp.where(slot_ref[...] == j, part, total)

    total = lax.fori_loop(0, wanted, one, jnp.zeros((rank, rows), f32))
    left, right = total[:, : rows // 2], total[:, rows // 2 :]
    keep_ref[...] = jnp.where(core == 0, left, right)
    give_ref[...] = jnp.where(core == 0, right, left)


def base_kernel(block_ref, *refs):
    *stacks, mine_ref, sib_ref, out_ref, weights, sems = refs
    count = weights.shape[0]
    columns = mine_ref.shape[2]

    def fetch(i, side):
        source = (mine_ref, sib_ref)[side].at[block_ref[i]]
        place = weights.at[i, :, side * columns : (side + 1) * columns]
        return pltpu.make_async_copy(source, place, sems.at[i, side])

    for i in range(count):
        for side in range(2):
            fetch(i, side).start()
    if len(stacks[0].shape) == 3 and stacks[0].shape[2] == columns:
        out_ref[...] = stacks[0][...]
        stacks = stacks[1:]
    else:
        out_ref[...] = jnp.zeros_like(out_ref)
    at = 0
    for stack in stacks:
        first = at

        def piece(i, carry):
            for side in range(2):
                fetch(first + i, side).wait()
            both = jnp.dot(stack[i], weights[first + i], preferred_element_type=f32)
            out_ref[0] += both[:, :columns]
            out_ref[1] += both[:, columns:]
            return carry

        lax.fori_loop(0, stack.shape[0], piece, 0)
        at += stack.shape[0]


def expand_kernel(panels_ref, scaled_ref, other_ref, slot_ref, here_ref, there_ref, out_ref):
    core = lax.rem(lax.axis_index("tensor"), 2)
    wanted, _, rank, columns = panels_ref.shape
    half = scaled_ref.shape[1]
    panel = jnp.concatenate([panels_ref[j, 1] for j in range(wanted)], axis=0)
    for part in range(2):
        mine = core == part
        scaled = jnp.where(mine, scaled_ref[...], other_ref[...])
        base = jnp.where(mine, here_ref[...], there_ref[...])
        slot = slot_ref[:, part * half : (part + 1) * half]
        delta = jnp.concatenate(
            [jnp.where(slot == j, scaled, jnp.zeros_like(scaled)) for j in range(wanted)], axis=0
        )
        total = base + lax.dot_general(delta, panel, (((0,), (0,)), ((), ())), preferred_element_type=f32)
        out_ref[part * half : (part + 1) * half, :] = total.astype(out_ref.dtype)


def own_kernel(hidden_ref, got_ref, out_ref):
    core = lax.rem(lax.axis_index("tensor"), 2)
    rows, feats = got_ref.shape
    mine = hidden_ref[pl.ds(pl.multiple_of(core * rows, rows), rows), :]
    got = got_ref[...]
    out_ref[:, :feats] = jnp.where(core == 0, mine, got)
    out_ref[:, feats:] = jnp.where(core == 0, got, mine)


def after(value, *earlier):
    return lax.optimization_barrier((value, *earlier))[0]


def per_device(hidden_rows, query_weight, down_panels, up_panels, store_index, requests, row_slot):
    rows, feats = hidden_rows.shape
    stored, rank, columns = down_panels.shape
    groups, wanted = requests.shape
    t = lax.axis_index("tensor")
    y, x, c = t // 8, (t // 2) % 4, t % 2
    slot_row = row_slot.reshape(1, rows)
    table = jnp.concatenate((requests.reshape(-1), store_index))

    with jax.named_scope("hidden_swap"):
        give = jnp.where(c == 0, hidden_rows[rows // 2 :], hidden_rows[: rows // 2])
        got = to_sibling(give)

    with jax.named_scope("panel_fetch"):
        spread = kernel_call(
            spread_kernel, jax.ShapeDtypeStruct((groups * wanted, 2, rank, columns), bf16),
            after(table, give), down_panels, up_panels,
        )
        panels = lax.psum_scatter(spread, "adapter", scatter_dimension=0, tiled=True)

    with jax.named_scope("hidden_first"):
        own_piece = kernel_call(
            own_kernel, jax.ShapeDtypeStruct((rows // 2, 2 * feats), bf16), hidden_rows, after(got, spread)
        )
        below = along_first(own_piece, 1)
        above = along_first(own_piece, -1)

    with jax.named_scope("weight_swap"):
        weight_sib = to_sibling(after(query_weight, own_piece))

    def blocks(firsts, second):
        out = []
        for first in firsts:
            sy = y + jnp.where(c == 0, second, first)
            sx = x + jnp.where(c == 0, first, second)
            out.append((sy % 4) * 4 + sx % 4)
        return out

    weight_shape = (16, 2 * feats, columns)
    weights = (query_weight.reshape(weight_shape), weight_sib.reshape(weight_shape))

    def add_base(total, *parts):
        order = sum([blocks(firsts, second) for _, firsts, second in parts], [])
        stacks = [stack for stack, _, _ in parts]
        if total is not None:
            stacks = [total] + stacks
        operands = [jnp.stack(order).astype(i32), *stacks, *weights]
        return kernel_call(
            base_kernel,
            jax.ShapeDtypeStruct((2, rows // 2, columns), f32),
            *operands,
            specs=[SMEM] + [VMEM] * len(stacks) + [ANY, ANY],
            scratch=[
                pltpu.VMEM((len(order), 2 * feats, 2 * columns), bf16),
                pltpu.SemaphoreType.DMA((len(order), 2)),
            ],
        )

    near_at, rest_at = (0, -1), (1, 2)
    with jax.named_scope("hidden_second"):
        near = jnp.stack((own_piece, below))
        beyond = along_first(below, 1)
        near_below, near_above = along_second(near, 1), along_second(near, -1)
        rest = jnp.stack((above, after(beyond, weight_sib)))
        rest_below, rest_above = along_second(rest, 1), along_second(rest, -1)
        near_below = after(near_below, rest)
        near_beyond = along_second(near_below, 1)
        near_above = after(near_above, near_below)
        rest_above = after(rest_above, near_above)
        rest_beyond = along_second(rest_above, -1)
    with jax.named_scope("shrink"):
        part = jax.ShapeDtypeStruct((rank, rows // 2), f32)
        keep, give = kernel_call(
            shrink_kernel, (part, part), after(panels, near_beyond, rest_beyond), hidden_rows, slot_row
        )
    with jax.named_scope("shrink_sum"):
        part = keep + to_sibling(give)
        pieces = along_x(part, 1), along_x(part, -1), along_x(part, 2)
    with jax.named_scope("base"):
        base = add_base(
            None, (after(near, part), near_at, 0), (rest, rest_at, 0), (near_below, near_at, -1), (near_above, near_at, 1)
        )
    with jax.named_scope("shrink_sum"):
        pieces = after(pieces, base)
        part = part + pieces[0] + pieces[1] + pieces[2]
        pieces = along_y(part, 1), along_y(part, -1), along_y(part, 2)
    with jax.named_scope("base"):
        base = add_base(
            after(base, part), (rest_below, rest_at, -1), (rest_above, rest_at, 1), (near_beyond, near_at, 2),
            (rest_beyond, rest_at, 2),
        )
    with jax.named_scope("shrink_sum"):
        pieces = after(pieces, base)
        part = part + pieces[0] + pieces[1] + pieces[2]
        scaled = (part * adapter_scale).astype(bf16)
        scaled_other = to_sibling(scaled)
    with jax.named_scope("base"):
        base_here = base[0]
        base_there = to_sibling(after(base[1], scaled))

    with jax.named_scope("expand"):
        return kernel_call(
            expand_kernel, jax.ShapeDtypeStruct((rows, columns), bf16),
            panels, scaled, scaled_other, slot_row, base_here, base_there,
        )


def solution(mesh):
    return jax.shard_map(
        per_device,
        mesh=mesh,
        in_specs=(
            P("adapter", "tensor"),
            P(None, "tensor"),
            P("adapter", None, "tensor"),
            P("adapter", None, "tensor"),
            P(),
            P(),
            P("adapter"),
        ),
        out_specs=P("adapter", "tensor"),
        check_vma=False,
    )
```

```python
import functools

import jax
import jax.numpy as jnp
from jax import lax
from jax.experimental import pallas as pl
from jax.experimental.pallas import tpu as pltpu
from jax.sharding import PartitionSpec as P

adapter_scale = 0.5
f32, bf16, i32 = jnp.float32, jnp.bfloat16, jnp.int32
NZ, NY, NX, NC = 8, 4, 4, 2
WANTED = 8
INDEX = NZ * WANTED
SMEM = pl.BlockSpec(memory_space=pltpu.SMEM)
VMEM = pl.BlockSpec(memory_space=pltpu.VMEM)
HBM = pl.BlockSpec(memory_space=pltpu.HBM)
ANY = pl.BlockSpec(memory_space=pl.ANY)


def kernel_call(kernel, out_shape, *operands, scratch=(), specs=None, limit=16 << 20, pin=True):
    specs = specs or [SMEM if v.dtype == i32 and v.size <= 256 else VMEM for v in operands]
    if pin:
        operands = [
            pltpu.with_memory_space_constraint(v, pltpu.VMEM) if spec is VMEM and v.size > 1024 else v
            for v, spec in zip(operands, specs)
        ]
        out_shape = jax.tree.map(lambda leaf: pltpu.VMEM(leaf.shape, leaf.dtype), out_shape)
    return pl.pallas_call(
        kernel,
        out_shape=out_shape,
        in_specs=specs,
        out_specs=jax.tree.map(lambda _: VMEM, out_shape),
        scratch_shapes=list(scratch),
        compiler_params=pltpu.CompilerParams(vmem_limit_bytes=limit),
    )(*operands)


def load_kernel(*refs):
    *sources, sems = refs
    sources, targets = sources[: len(sources) // 2], sources[len(sources) // 2 :]
    loads = [pltpu.make_async_copy(a, b, sems.at[i]) for i, (a, b) in enumerate(zip(sources, targets))]
    for load in loads:
        load.start()
    for load in loads:
        load.wait()


def send(value, to):
    pairs = []
    for z in range(NZ):
        for y in range(NY):
            for x in range(NX):
                for c in range(NC):
                    tz, ty, tx, tc = to(z, y, x, c)
                    here = ((z * NY + y) * NX + x) * NC + c
                    there = ((tz % NZ * NY + ty % NY) * NX + tx % NX) * NC + tc
                    pairs.append((here, there))
    return lax.ppermute(value, ("adapter", "tensor"), pairs)


def to_sibling(value):
    return send(value, lambda z, y, x, c: (z, y, x, 1 - c))


def along_z(value, cross=0):
    return send(value, lambda z, y, x, c: (z + 1 - 2 * c, y, x, c ^ cross))


def along_x(value, step):
    return send(value, lambda z, y, x, c: (z, y, x + step, c))


def along_y(value, step):
    return send(value, lambda z, y, x, c: (z, y + step, x, c))


def along_first(value, step):
    return send(value, lambda z, y, x, c: (z, y + step * c, x + step * (1 - c), c))


def along_second(value, step):
    return send(value, lambda z, y, x, c: (z, y + step * (1 - c), x + step * c, c))


def slot_of(table_ref, group, at):
    return table_ref[INDEX + table_ref[group * WANTED + at]]


def panel_of(table_ref, group, at, stored):
    local = slot_of(table_ref, group, at) - lax.axis_index("adapter") * stored
    return jnp.clip(local, 0, stored - 1), (local >= 0) & (local < stored)


def ahead(distance):
    sign = 1 - 2 * lax.rem(lax.axis_index("tensor"), 2)
    return lax.rem(lax.axis_index("adapter") + sign * distance + NZ, NZ)


def fill_kernel(blocks, stores_at, table_ref, *refs):
    inputs, stores, outs = refs[: stores_at[0]], refs[stores_at[0] : stores_at[1]], refs[stores_at[1] :]
    core = lax.rem(lax.axis_index("tensor"), 2)
    for kind, side, distance, width, source, (target, place) in blocks:
        store = stores[2 * kind + side]
        group = ahead(distance)
        first = core * width if width < WANTED else 0

        def slot(j, carry, store=store, group=group, first=first, source=source, out=outs[target], place=place):
            at, here = panel_of(table_ref, group, first + j, store.shape[0])
            panel = store[at]
            if source is None:
                old = jnp.zeros_like(panel)
            else:
                array, begin, held = source
                there = j - core * held if held < WANTED else j
                old = inputs[array][begin + jnp.clip(there, 0, held - 1)]
                if held < WANTED:
                    old = jnp.where((there >= 0) & (there < held), old, jnp.zeros_like(old))
            out[place + j] = jnp.where(here, panel, old)
            return carry

        lax.fori_loop(0, width, slot, 0, unroll=4)


def joined(table_ref, j, same_ref, cross_ref, store_ref):
    stored = store_ref.shape[0]
    core = lax.rem(lax.axis_index("tensor"), 2)
    group = lax.axis_index("adapter")
    storage = slot_of(table_ref, group, j)
    behind = lax.rem(group - storage // stored + NZ, NZ)
    below = (behind < NZ // 2) | ((behind == NZ // 2) & (j < WANTED // 2))
    own = store_ref[jnp.clip(storage - group * stored, 0, stored - 1)]
    return jnp.where(behind == 0, own, jnp.where(below == (core == 0), same_ref[j], cross_ref[j]))


def join_kernel(table_ref, same_ref, cross_ref, store_ref, out_ref):
    def one(j, carry):
        out_ref[j] = joined(table_ref, j, same_ref, cross_ref, store_ref)
        return carry

    lax.fori_loop(0, out_ref.shape[0], one, 0)


def shrink_kernel(table_ref, same_ref, cross_ref, store_ref, turned_ref, slot_ref, keep_ref, give_ref, panels, parts):
    wanted, rank, feats = panels.shape
    half = turned_ref.shape[1] // 2
    core = lax.rem(lax.axis_index("tensor"), 2)

    def one(j, carry):
        panels[j] = joined(table_ref, j, same_ref, cross_ref, store_ref)
        return carry

    lax.fori_loop(0, wanted, one, 0)
    flat = panels[...].reshape(wanted * rank, feats)
    parts[...] = jnp.dot(flat, turned_ref[...], preferred_element_type=f32)
    for side in range(2):
        columns = slice(side * half, (side + 1) * half)
        slot = slot_ref[:, columns]
        total = jnp.zeros((rank, half), f32)
        for j in range(wanted):
            total = jnp.where(slot == j, parts[j * rank : (j + 1) * rank, columns], total)

        @pl.when(core == side)
        def _():
            keep_ref[...] = total

        @pl.when(core != side)
        def _():
            give_ref[...] = total


def base_kernel(block_ref, *refs):
    *stacks, mine_ref, sib_ref, out_ref, lefts, weights, sems = refs
    columns = mine_ref.shape[2]
    total = stacks.pop(0) if len(stacks[0].shape) == 3 and stacks[0].shape[2] == columns else None
    pieces = [stack.at[i] for stack in stacks for i in range(stack.shape[0])]

    def fetch(i, side):
        source = (mine_ref, sib_ref)[side].at[block_ref[i]]
        place = weights.at[i, :, side * columns : (side + 1) * columns]
        return pltpu.make_async_copy(source, place, sems.at[i, side])

    def fetch_left(i):
        return pltpu.make_async_copy(pieces[i] if isinstance(i, int) else pieces[0], lefts.at[i], sems.at[i, 2])

    for i in range(len(pieces)):
        fetch_left(i).start()
        for side in range(2):
            fetch(i, side).start()
    out_ref[...] = jnp.zeros_like(out_ref) if total is None else total[...]

    def piece(i, carry):
        fetch_left(i).wait()
        for side in range(2):
            fetch(i, side).wait()
        both = jnp.dot(lefts[i], weights[i], preferred_element_type=f32)
        out_ref[0] += both[:, :columns]
        out_ref[1] += both[:, columns:]
        return carry

    lax.fori_loop(0, len(pieces), piece, 0)


def expand_kernel(panels_ref, scaled_ref, other_ref, slot_ref, here_ref, there_ref, out_ref):
    core = lax.rem(lax.axis_index("tensor"), 2)
    wanted, rank, columns = panels_ref.shape
    half = scaled_ref.shape[1]
    panel = panels_ref[...].reshape(wanted * rank, columns)
    for part in range(2):
        mine = core == part
        scaled = jnp.where(mine, scaled_ref[...], other_ref[...])
        base = jnp.where(mine, here_ref[...], there_ref[...])
        slot = slot_ref[:, part * half : (part + 1) * half]
        delta = jnp.concatenate(
            [jnp.where(slot == j, scaled, jnp.zeros_like(scaled)) for j in range(wanted)], axis=0
        )
        total = base + lax.dot_general(delta, panel, (((0,), (0,)), ((), ())), preferred_element_type=f32)
        out_ref[part * half : (part + 1) * half, :] = total.astype(out_ref.dtype)


def own_kernel(hidden_ref, got_ref, out_ref, turned_ref):
    core = lax.rem(lax.axis_index("tensor"), 2)
    rows, feats = hidden_ref.shape
    half = pl.ds(pl.multiple_of(core * (rows // 2), rows // 2), rows // 2)
    mine, got = hidden_ref[half, :], got_ref[half, :]
    out_ref[:, :feats] = jnp.where(core == 0, mine, got)
    out_ref[:, feats:] = jnp.where(core == 0, got, mine)
    turned_ref[...] = hidden_ref[...].T


def after(value, *earlier):
    return lax.optimization_barrier((value, *earlier))[0]


def per_device(hidden_rows, query_weight, down_panels, up_panels, store_index, requests, row_slot):
    rows, feats = hidden_rows.shape
    stored, rank, columns = down_panels.shape
    groups, wanted = requests.shape
    t = lax.axis_index("tensor")
    y, x, c = t // 8, (t // 2) % 4, t % 2
    slot_row = row_slot.reshape(1, rows)
    table = jnp.concatenate((requests.reshape(-1), store_index))

    down_sib = to_sibling(down_panels)
    got = to_sibling(hidden_rows)
    sources = (down_panels, up_panels, hidden_rows)
    down_panels, up_panels_here, hidden_rows = kernel_call(
        load_kernel, tuple(jax.ShapeDtypeStruct(v.shape, bf16) for v in sources),
        *[pltpu.with_memory_space_constraint(v, pltpu.HBM) for v in sources],
        specs=[ANY] * 3, scratch=[pltpu.SemaphoreType.DMA((3,))],
    )

    def step(parts, sizes, inputs, *earlier):
        stores = (down_panels, down_sib) + ((up_panels_here, up_sib) if any(part[0] for part in parts) else ())
        inputs = [after(value, *earlier) for value in inputs]
        ends = (len(inputs), len(inputs) + len(stores))
        return kernel_call(
            functools.partial(fill_kernel, parts, ends),
            tuple(jax.ShapeDtypeStruct((size, rank, columns), bf16) for size in sizes),
            after(table, *earlier), *inputs, *stores,
        )

    def blocks(firsts, second):
        out = []
        for first in firsts:
            sy = y + jnp.where(c == 0, second, first)
            sx = x + jnp.where(c == 0, first, second)
            out.append((sy % 4) * 4 + sx % 4)
        return out

    weight_shape = (16, 2 * feats, columns)

    def add_base(total, *parts):
        order = sum([blocks(firsts, second) for _, firsts, second in parts], [])
        stacks = [stack for stack, _, _ in parts]
        operands = ([] if total is None else [total]) + stacks
        return kernel_call(
            base_kernel,
            jax.ShapeDtypeStruct((2, rows // 2, columns), f32),
            jnp.stack(order).astype(i32), *operands,
            pltpu.with_memory_space_constraint(query_weight.reshape(weight_shape), pltpu.HBM),
            weight_sib.reshape(weight_shape),
            specs=[SMEM] + ([] if total is None else [VMEM]) + [ANY] * (len(stacks) + 2), pin=False,
            scratch=[
                pltpu.VMEM((len(order), rows // 2, 2 * feats), bf16),
                pltpu.VMEM((len(order), 2 * feats, 2 * columns), bf16),
                pltpu.SemaphoreType.DMA((len(order), 3)),
            ],
        )

    near_at, rest_at = (0, -1), (1, 2)
    few, all_of = wanted // 2, wanted
    (ring1,) = step(
        [(0, 0, 4, few, None, (0, 0)), (0, 1, 4, few, None, (0, few))], (2 * few,), [], down_sib
    )
    hop1 = along_z(ring1)
    own_piece, turned = kernel_call(
        own_kernel,
        (jax.ShapeDtypeStruct((rows // 2, 2 * feats), bf16), jax.ShapeDtypeStruct((feats, rows), bf16)),
        hidden_rows, after(got, ring1),
    )
    below, above = along_first(own_piece, 1), along_first(own_piece, -1)
    up_sib = to_sibling(after(up_panels, own_piece))
    weight_sib = to_sibling(after(query_weight, own_piece))

    (ring2,) = step(
        [
            (0, 0, 3, all_of, (0, 0, few), (0, 0)), (0, 1, 3, all_of, (0, few, few), (0, all_of)),
            (1, 0, 4, few, None, (0, 2 * all_of)), (1, 1, 4, few, None, (0, 2 * all_of + few)),
        ],
        (3 * all_of,), [hop1], own_piece, up_sib, below, above,
    )
    hop2 = along_z(ring2)
    below, above = after((below, above), ring2)
    near = jnp.stack((own_piece, below))
    near_below, near_above, beyond = along_second(near, 1), along_second(near, -1), along_first(below, 1)

    (ring3,) = step(
        [
            (0, 0, 2, all_of, (0, 0, all_of), (0, 0)), (0, 1, 2, all_of, (0, all_of, all_of), (0, all_of)),
            (1, 0, 3, all_of, (0, 2 * all_of, few), (0, 2 * all_of)),
            (1, 1, 3, all_of, (0, 2 * all_of + few, few), (0, 3 * all_of)),
        ],
        (4 * all_of,), [hop2], near, beyond,
    )
    hop3 = along_z(ring3)
    near_below, near_above, beyond = after((near_below, near_above, beyond), ring3)
    rest = jnp.stack((above, beyond))
    rest_below, rest_above, near_beyond = along_second(rest, 1), along_second(rest, -1), along_second(near_below, 1)
    base = add_base(None, (after(near, rest), near_at, 0), (near_below, near_at, -1), (near_above, near_at, 1))

    ring4, ring4_cross = step(
        [
            (0, 0, 1, all_of, (0, 0, all_of), (0, 0)), (0, 1, 1, all_of, (0, all_of, all_of), (1, 0)),
            (1, 0, 2, all_of, (0, 2 * all_of, all_of), (0, all_of)),
            (1, 1, 2, all_of, (0, 3 * all_of, all_of), (0, 2 * all_of)),
        ],
        (3 * all_of, all_of), [hop3], base,
    )
    hop4, down_cross = along_z(ring4), along_z(ring4_cross, 1)
    rest_below, rest_above = after((rest_below, rest_above), ring4)
    rest_beyond = along_second(rest_above, -1)
    base = add_base(base, (rest, rest_at, 0), (rest_below, rest_at, -1), (rest_above, rest_at, 1))

    with jax.named_scope("shrink"):
        part = jax.ShapeDtypeStruct((rank, rows // 2), f32)
        keep, give = kernel_call(
            shrink_kernel, (part, part), table, after(hop4, base), down_cross, down_panels, turned, slot_row,
            scratch=[pltpu.VMEM((wanted, rank, columns), bf16), pltpu.VMEM((wanted * rank, rows), f32)],
        )
    with jax.named_scope("shrink_sum"):
        part = keep + to_sibling(give)
        pieces = along_x(part, 1), along_x(part, -1), along_x(part, 2)
    up_to_same, up_to_cross = step(
        [
            (1, 0, 1, all_of, (0, all_of, all_of), (0, 0)), (1, 1, 1, all_of, (0, 2 * all_of, all_of), (1, 0)),
        ],
        (all_of, all_of), [hop4], part,
    )
    up_same, up_cross = along_z(up_to_same), along_z(up_to_cross, 1)
    with jax.named_scope("shrink_sum"):
        pieces = after(pieces, up_to_same)
        part = part + pieces[0] + pieces[1] + pieces[2]
        pieces = along_y(part, 1), along_y(part, -1), along_y(part, 2)
    base = add_base(after(base, part), (near_beyond, near_at, 2), (rest_beyond, rest_at, 2))
    up_here = kernel_call(
        join_kernel, jax.ShapeDtypeStruct((wanted, rank, columns), bf16), table, after(up_same, base), up_cross, up_panels_here
    )
    with jax.named_scope("shrink_sum"):
        pieces = after(pieces, up_here)
        part = part + pieces[0] + pieces[1] + pieces[2]
        scaled = (part * adapter_scale).astype(bf16)
        scaled_other = to_sibling(scaled)
    with jax.named_scope("base"):
        base_here = base[0]
        base_there = to_sibling(after(base[1], scaled))

    with jax.named_scope("expand"):
        return kernel_call(
            expand_kernel, jax.ShapeDtypeStruct((rows, columns), bf16),
            up_here, scaled, scaled_other, slot_row, base_here, base_there,
        )


def solution(mesh):
    return jax.shard_map(
        per_device,
        mesh=mesh,
        in_specs=(
            P("adapter", "tensor"),
            P(None, "tensor"),
            P("adapter", None, "tensor"),
            P("adapter", None, "tensor"),
            P(),
            P(),
            P("adapter"),
        ),
        out_specs=P("adapter", "tensor"),
        check_vma=False,
    )
```

```python
import functools

import jax
import jax.numpy as jnp
from jax import lax
from jax.experimental import pallas as pl
from jax.experimental.pallas import tpu as pltpu
from jax.sharding import PartitionSpec as P

adapter_scale = 0.5
f32, bf16, i32 = jnp.float32, jnp.bfloat16, jnp.int32
NZ, NY, NX, NC = 8, 4, 4, 2
WANTED = 8
INDEX = NZ * WANTED
SMEM = pl.BlockSpec(memory_space=pltpu.SMEM)
VMEM = pl.BlockSpec(memory_space=pltpu.VMEM)
HBM = pl.BlockSpec(memory_space=pltpu.HBM)
ANY = pl.BlockSpec(memory_space=pl.ANY)


def kernel_call(kernel, out_shape, *operands, scratch=(), specs=None, limit=16 << 20, pin=True):
    specs = specs or [SMEM if v.dtype == i32 and v.size <= 256 else VMEM for v in operands]
    if pin:
        operands = [
            pltpu.with_memory_space_constraint(v, pltpu.VMEM) if spec is VMEM and v.size > 1024 else v
            for v, spec in zip(operands, specs)
        ]
        out_shape = jax.tree.map(lambda leaf: pltpu.VMEM(leaf.shape, leaf.dtype), out_shape)
    return pl.pallas_call(
        kernel,
        out_shape=out_shape,
        in_specs=specs,
        out_specs=jax.tree.map(lambda _: VMEM, out_shape),
        scratch_shapes=list(scratch),
        compiler_params=pltpu.CompilerParams(vmem_limit_bytes=limit),
    )(*operands)


def load_kernel(*refs):
    *sources, sems = refs
    sources, targets = sources[: len(sources) // 2], sources[len(sources) // 2 :]
    loads = [pltpu.make_async_copy(a, b, sems.at[i]) for i, (a, b) in enumerate(zip(sources, targets))]
    for load in loads:
        load.start()
    for load in loads:
        load.wait()


def send(value, to):
    pairs = []
    for z in range(NZ):
        for y in range(NY):
            for x in range(NX):
                for c in range(NC):
                    tz, ty, tx, tc = to(z, y, x, c)
                    here = ((z * NY + y) * NX + x) * NC + c
                    there = ((tz % NZ * NY + ty % NY) * NX + tx % NX) * NC + tc
                    pairs.append((here, there))
    return lax.ppermute(value, ("adapter", "tensor"), pairs)


def to_sibling(value):
    return send(value, lambda z, y, x, c: (z, y, x, 1 - c))


def along_z(value, cross=0):
    return send(value, lambda z, y, x, c: (z + 1 - 2 * c, y, x, c ^ cross))


def along_x(value, step):
    return send(value, lambda z, y, x, c: (z, y, x + step, c))


def along_y(value, step):
    return send(value, lambda z, y, x, c: (z, y + step, x, c))


def along_first(value, step):
    return send(value, lambda z, y, x, c: (z, y + step * c, x + step * (1 - c), c))


def along_second(value, step):
    return send(value, lambda z, y, x, c: (z, y + step * (1 - c), x + step * c, c))


def slot_of(table_ref, group, at):
    return table_ref[INDEX + table_ref[group * WANTED + at]]


def panel_of(table_ref, group, at, stored):
    local = slot_of(table_ref, group, at) - lax.axis_index("adapter") * stored
    return jnp.clip(local, 0, stored - 1), (local >= 0) & (local < stored)


def ahead(distance):
    sign = 1 - 2 * lax.rem(lax.axis_index("tensor"), 2)
    return lax.rem(lax.axis_index("adapter") + sign * distance + NZ, NZ)


def fill_kernel(blocks, stores_at, table_ref, *refs):
    inputs, stores, outs = refs[: stores_at[0]], refs[stores_at[0] : stores_at[1]], refs[stores_at[1] :]
    core = lax.rem(lax.axis_index("tensor"), 2)
    for kind, side, distance, width, source, (target, place) in blocks:
        store = stores[2 * kind + side]
        group = ahead(distance)
        first = core * width if width < WANTED else 0

        def slot(j, carry, store=store, group=group, first=first, source=source, out=outs[target], place=place):
            at, here = panel_of(table_ref, group, first + j, store.shape[0])
            panel = store[at]
            if source is None:
                old = jnp.zeros_like(panel)
            else:
                array, begin, held = source
                there = j - core * held if held < WANTED else j
                old = inputs[array][begin + jnp.clip(there, 0, held - 1)]
                if held < WANTED:
                    old = jnp.where((there >= 0) & (there < held), old, jnp.zeros_like(old))
            out[place + j] = jnp.where(here, panel, old)
            return carry

        lax.fori_loop(0, width, slot, 0, unroll=4)


def joined(table_ref, j, same_ref, cross_ref, store_ref):
    stored = store_ref.shape[0]
    core = lax.rem(lax.axis_index("tensor"), 2)
    group = lax.axis_index("adapter")
    storage = slot_of(table_ref, group, j)
    behind = lax.rem(group - storage // stored + NZ, NZ)
    below = (behind < NZ // 2) | ((behind == NZ // 2) & (j < WANTED // 2))
    own = store_ref[jnp.clip(storage - group * stored, 0, stored - 1)]
    return jnp.where(behind == 0, own, jnp.where(below == (core == 0), same_ref[j], cross_ref[j]))


def join_kernel(table_ref, same_ref, cross_ref, store_ref, out_ref):
    def one(j, carry):
        out_ref[j] = joined(table_ref, j, same_ref, cross_ref, store_ref)
        return carry

    lax.fori_loop(0, out_ref.shape[0], one, 0)


def shrink_kernel(table_ref, here_ref, other_ref, mine_ref, sib_ref, turned_ref, slot_ref, out_ref, panels, parts):
    rank, half = out_ref.shape
    stored = mine_ref.shape[0]
    core = lax.rem(lax.axis_index("tensor"), 2)
    group = lax.axis_index("adapter")
    feats = mine_ref.shape[2]

    def one(j, carry):
        storage = slot_of(table_ref, group, j)
        behind = lax.rem(group - storage // stored + NZ, NZ)
        below = (behind < NZ // 2) | ((behind == NZ // 2) & (j < WANTED // 2))
        at = jnp.clip(storage - group * stored, 0, stored - 1)
        for side, store in enumerate((mine_ref, sib_ref)):
            came = jnp.where(below == (core == 0), here_ref[side * WANTED + j], other_ref[(1 - side) * WANTED + j])
            panels[j, :, side * feats : (side + 1) * feats] = jnp.where(behind == 0, store[at], came)
        return carry

    lax.fori_loop(0, WANTED, one, 0, unroll=2)
    flat = panels[...].reshape(WANTED * rank, 2 * feats)
    parts[...] = jnp.dot(flat, turned_ref[...], preferred_element_type=f32)
    slot = slot_ref[:, pl.ds(pl.multiple_of(core * half, 128), half)]
    total = jnp.zeros((rank, half), f32)
    for j in range(WANTED):
        total = jnp.where(slot == j, parts[j * rank : (j + 1) * rank, :], total)
    out_ref[...] = total


def base_kernel(block_ref, *refs):
    *stacks, mine_ref, sib_ref, out_ref, lefts, weights, sems = refs
    columns = mine_ref.shape[2]
    total = stacks.pop(0) if len(stacks[0].shape) == 3 and stacks[0].shape[2] == columns else None
    pieces = [stack.at[i] for stack in stacks for i in range(stack.shape[0])]

    def fetch(i, side):
        source = (mine_ref, sib_ref)[side].at[block_ref[i]]
        place = weights.at[i, :, side * columns : (side + 1) * columns]
        return pltpu.make_async_copy(source, place, sems.at[i, side])

    def fetch_left(i):
        return pltpu.make_async_copy(pieces[i] if isinstance(i, int) else pieces[0], lefts.at[i], sems.at[i, 2])

    for i in range(len(pieces)):
        fetch_left(i).start()
        for side in range(2):
            fetch(i, side).start()
    out_ref[...] = jnp.zeros_like(out_ref) if total is None else total[...]

    def piece(i, carry):
        fetch_left(i).wait()
        for side in range(2):
            fetch(i, side).wait()
        both = jnp.dot(lefts[i], weights[i], preferred_element_type=f32)
        out_ref[0] += both[:, :columns]
        out_ref[1] += both[:, columns:]
        return carry

    lax.fori_loop(0, len(pieces), piece, 0)


def expand_kernel(panels_ref, scaled_ref, other_ref, slot_ref, here_ref, there_ref, out_ref):
    core = lax.rem(lax.axis_index("tensor"), 2)
    wanted, rank, columns = panels_ref.shape
    half = scaled_ref.shape[1]
    panel = panels_ref[...].reshape(wanted * rank, columns)
    for part in range(2):
        mine = core == part
        scaled = jnp.where(mine, scaled_ref[...], other_ref[...])
        base = jnp.where(mine, here_ref[...], there_ref[...])
        slot = slot_ref[:, part * half : (part + 1) * half]
        delta = jnp.concatenate(
            [jnp.where(slot == j, scaled, jnp.zeros_like(scaled)) for j in range(wanted)], axis=0
        )
        total = base + lax.dot_general(delta, panel, (((0,), (0,)), ((), ())), preferred_element_type=f32)
        out_ref[part * half : (part + 1) * half, :] = total.astype(out_ref.dtype)


def own_kernel(hidden_ref, got_ref, out_ref, turned_ref):
    core = lax.rem(lax.axis_index("tensor"), 2)
    rows, feats = hidden_ref.shape
    half = pl.ds(pl.multiple_of(core * (rows // 2), rows // 2), rows // 2)
    mine, got = hidden_ref[half, :], got_ref[half, :]
    out_ref[:, :feats] = jnp.where(core == 0, mine, got)
    out_ref[:, feats:] = jnp.where(core == 0, got, mine)
    turned_ref[:feats, :] = mine.T
    turned_ref[feats:, :] = got.T


def after(value, *earlier):
    return lax.optimization_barrier((value, *earlier))[0]


def per_device(hidden_rows, query_weight, down_panels, up_panels, store_index, requests, row_slot):
    rows, feats = hidden_rows.shape
    stored, rank, columns = down_panels.shape
    groups, wanted = requests.shape
    t = lax.axis_index("tensor")
    y, x, c = t // 8, (t // 2) % 4, t % 2
    slot_row = row_slot.reshape(1, rows)
    table = jnp.concatenate((requests.reshape(-1), store_index))

    down_sib = to_sibling(down_panels)
    got = to_sibling(hidden_rows)
    sources = (down_panels, up_panels, hidden_rows)
    down_panels, up_panels_here, hidden_rows = kernel_call(
        load_kernel, tuple(jax.ShapeDtypeStruct(v.shape, bf16) for v in sources),
        *[pltpu.with_memory_space_constraint(v, pltpu.HBM) for v in sources],
        specs=[ANY] * 3, scratch=[pltpu.SemaphoreType.DMA((3,))],
    )

    def step(parts, sizes, inputs, *earlier):
        stores = (down_panels, down_sib) + ((up_panels_here, up_sib) if any(part[0] for part in parts) else ())
        inputs = [after(value, *earlier) for value in inputs]
        ends = (len(inputs), len(inputs) + len(stores))
        return kernel_call(
            functools.partial(fill_kernel, parts, ends),
            tuple(jax.ShapeDtypeStruct((size, rank, columns), bf16) for size in sizes),
            after(table, *earlier), *inputs, *stores,
        )

    def blocks(firsts, second):
        out = []
        for first in firsts:
            sy = y + jnp.where(c == 0, second, first)
            sx = x + jnp.where(c == 0, first, second)
            out.append((sy % 4) * 4 + sx % 4)
        return out

    weight_shape = (16, 2 * feats, columns)

    def add_base(total, *parts):
        order = sum([blocks(firsts, second) for _, firsts, second in parts], [])
        stacks = [stack for stack, _, _ in parts]
        operands = ([] if total is None else [total]) + stacks
        return kernel_call(
            base_kernel,
            jax.ShapeDtypeStruct((2, rows // 2, columns), f32),
            jnp.stack(order).astype(i32), *operands,
            pltpu.with_memory_space_constraint(query_weight.reshape(weight_shape), pltpu.HBM),
            weight_sib.reshape(weight_shape),
            specs=[SMEM] + ([] if total is None else [VMEM]) + [ANY] * (len(stacks) + 2), pin=False,
            scratch=[
                pltpu.VMEM((len(order), rows // 2, 2 * feats), bf16),
                pltpu.VMEM((len(order), 2 * feats, 2 * columns), bf16),
                pltpu.SemaphoreType.DMA((len(order), 3)),
            ],
        )

    near_at, rest_at = (0, -1), (1, 2)
    few, all_of = wanted // 2, wanted
    (ring1,) = step(
        [(0, 0, 4, few, None, (0, 0)), (0, 1, 4, few, None, (0, few))], (2 * few,), [], down_sib
    )
    hop1 = along_z(ring1)
    own_piece, turned = kernel_call(
        own_kernel,
        (jax.ShapeDtypeStruct((rows // 2, 2 * feats), bf16), jax.ShapeDtypeStruct((2 * feats, rows // 2), bf16)),
        hidden_rows, after(got, ring1),
    )
    below, above = along_first(own_piece, 1), along_first(own_piece, -1)
    up_sib = to_sibling(after(up_panels, own_piece))
    weight_sib = to_sibling(after(query_weight, own_piece))

    (ring2,) = step(
        [
            (0, 0, 3, all_of, (0, 0, few), (0, 0)), (0, 1, 3, all_of, (0, few, few), (0, all_of)),
            (1, 0, 4, few, None, (0, 2 * all_of)), (1, 1, 4, few, None, (0, 2 * all_of + few)),
        ],
        (3 * all_of,), [hop1], own_piece, up_sib, below, above,
    )
    hop2 = along_z(ring2)
    below, above = after((below, above), ring2)
    near = jnp.stack((own_piece, below))
    near_below, near_above, beyond = along_second(near, 1), along_second(near, -1), along_first(below, 1)

    (ring3,) = step(
        [
            (0, 0, 2, all_of, (0, 0, all_of), (0, 0)), (0, 1, 2, all_of, (0, all_of, all_of), (0, all_of)),
            (1, 0, 3, all_of, (0, 2 * all_of, few), (0, 2 * all_of)),
            (1, 1, 3, all_of, (0, 2 * all_of + few, few), (0, 3 * all_of)),
        ],
        (4 * all_of,), [hop2], near, beyond,
    )
    hop3 = along_z(ring3)
    near_below, near_above, beyond = after((near_below, near_above, beyond), ring3)
    rest = jnp.stack((above, beyond))
    rest_below, rest_above, near_beyond = along_second(rest, 1), along_second(rest, -1), along_second(near_below, 1)
    base = add_base(None, (after(near, rest), near_at, 0), (near_below, near_at, -1), (near_above, near_at, 1))

    ring4, ring4_up = step(
        [
            (0, 0, 1, all_of, (0, 0, all_of), (0, 0)), (0, 1, 1, all_of, (0, all_of, all_of), (0, all_of)),
            (1, 0, 2, all_of, (0, 2 * all_of, all_of), (1, 0)), (1, 1, 2, all_of, (0, 3 * all_of, all_of), (1, all_of)),
        ],
        (2 * all_of, 2 * all_of), [hop3], base,
    )
    hop4, hop4_up = along_z(ring4), along_z(ring4_up)
    rest_below, rest_above = after((rest_below, rest_above), ring4)
    rest_beyond = along_second(rest_above, -1)
    base = add_base(
        base, (rest, rest_at, 0), (rest_below, rest_at, -1), (rest_above, rest_at, 1),
    )

    with jax.named_scope("shrink"):
        hop4 = after(hop4, base)
        part = kernel_call(
            shrink_kernel, jax.ShapeDtypeStruct((rank, rows // 2), f32),
            table, hop4, to_sibling(hop4), down_panels, down_sib, turned, slot_row,
            scratch=[pltpu.VMEM((wanted, rank, 2 * feats), bf16), pltpu.VMEM((wanted * rank, rows // 2), f32)],
        )
    with jax.named_scope("shrink_sum"):
        part = after(part, near_beyond, rest_beyond)
        pieces = along_x(part, 1), along_x(part, -1), along_x(part, 2)
    up_to_same, up_to_cross = step(
        [
            (1, 0, 1, all_of, (0, 0, all_of), (0, 0)), (1, 1, 1, all_of, (0, all_of, all_of), (1, 0)),
        ],
        (all_of, all_of), [hop4_up], part,
    )
    up_same, up_cross = along_z(up_to_same), along_z(up_to_cross, 1)
    with jax.named_scope("shrink_sum"):
        pieces = after(pieces, up_to_same)
        part = part + pieces[0] + pieces[1] + pieces[2]
        pieces = along_y(part, 1), along_y(part, -1), along_y(part, 2)
    base = add_base(after(base, part), (near_beyond, near_at, 2), (rest_beyond, rest_at, 2))
    up_here = kernel_call(
        join_kernel, jax.ShapeDtypeStruct((wanted, rank, columns), bf16), table, after(up_same, base), up_cross, up_panels_here
    )
    with jax.named_scope("shrink_sum"):
        pieces = after(pieces, up_here)
        part = part + pieces[0] + pieces[1] + pieces[2]
        scaled = (part * adapter_scale).astype(bf16)
        scaled_other = to_sibling(scaled)
    with jax.named_scope("base"):
        base_here = base[0]
        base_there = to_sibling(after(base[1], scaled))

    with jax.named_scope("expand"):
        return kernel_call(
            expand_kernel, jax.ShapeDtypeStruct((rows, columns), bf16),
            up_here, scaled, scaled_other, slot_row, base_here, base_there,
        )


def solution(mesh):
    return jax.shard_map(
        per_device,
        mesh=mesh,
        in_specs=(
            P("adapter", "tensor"),
            P(None, "tensor"),
            P("adapter", None, "tensor"),
            P("adapter", None, "tensor"),
            P(),
            P(),
            P("adapter"),
        ),
        out_specs=P("adapter", "tensor"),
        check_vma=False,
    )
```

```python
import functools

import jax
import jax.numpy as jnp
from jax import lax
from jax.experimental import pallas as pl
from jax.experimental.pallas import tpu as pltpu
from jax.sharding import PartitionSpec as P

adapter_scale = 0.5
f32, bf16, i32 = jnp.float32, jnp.bfloat16, jnp.int32
NZ, NY, NX, NC = 8, 4, 4, 2
WANTED = 8
INDEX = NZ * WANTED
SMEM = pl.BlockSpec(memory_space=pltpu.SMEM)
VMEM = pl.BlockSpec(memory_space=pltpu.VMEM)
HBM = pl.BlockSpec(memory_space=pltpu.HBM)
ANY = pl.BlockSpec(memory_space=pl.ANY)


def kernel_call(kernel, out_shape, *operands, scratch=(), specs=None, limit=16 << 20, pin=True):
    specs = specs or [SMEM if v.dtype == i32 and v.size <= 256 else VMEM for v in operands]
    if pin:
        operands = [
            pltpu.with_memory_space_constraint(v, pltpu.VMEM) if spec is VMEM and v.size > 1024 else v
            for v, spec in zip(operands, specs)
        ]
        out_shape = jax.tree.map(lambda leaf: pltpu.VMEM(leaf.shape, leaf.dtype), out_shape)
    return pl.pallas_call(
        kernel,
        out_shape=out_shape,
        in_specs=specs,
        out_specs=jax.tree.map(lambda _: VMEM, out_shape),
        scratch_shapes=list(scratch),
        compiler_params=pltpu.CompilerParams(vmem_limit_bytes=limit),
    )(*operands)


def load_kernel(*refs):
    *sources, sems = refs
    sources, targets = sources[: len(sources) // 2], sources[len(sources) // 2 :]
    loads = [pltpu.make_async_copy(a, b, sems.at[i]) for i, (a, b) in enumerate(zip(sources, targets))]
    for load in loads:
        load.start()
    for load in loads:
        load.wait()


def send(value, to):
    pairs = []
    for z in range(NZ):
        for y in range(NY):
            for x in range(NX):
                for c in range(NC):
                    tz, ty, tx, tc = to(z, y, x, c)
                    here = ((z * NY + y) * NX + x) * NC + c
                    there = ((tz % NZ * NY + ty % NY) * NX + tx % NX) * NC + tc
                    pairs.append((here, there))
    return lax.ppermute(value, ("adapter", "tensor"), pairs)


def to_sibling(value):
    return send(value, lambda z, y, x, c: (z, y, x, 1 - c))


def along_z(value, cross=0):
    return send(value, lambda z, y, x, c: (z + 1 - 2 * c, y, x, c ^ cross))


def along_x(value, step):
    return send(value, lambda z, y, x, c: (z, y, x + step, c))


def along_y(value, step):
    return send(value, lambda z, y, x, c: (z, y + step, x, c))


def along_first(value, step):
    return send(value, lambda z, y, x, c: (z, y + step * c, x + step * (1 - c), c))


def along_second(value, step):
    return send(value, lambda z, y, x, c: (z, y + step * (1 - c), x + step * c, c))


def slot_of(table_ref, group, at):
    return table_ref[INDEX + table_ref[group * WANTED + at]]


def panel_of(table_ref, group, at, stored):
    local = slot_of(table_ref, group, at) - lax.axis_index("adapter") * stored
    return jnp.clip(local, 0, stored - 1), (local >= 0) & (local < stored)


def ahead(distance):
    sign = 1 - 2 * lax.rem(lax.axis_index("tensor"), 2)
    return lax.rem(lax.axis_index("adapter") + sign * distance + NZ, NZ)


def fill_kernel(blocks, stores_at, table_ref, *refs):
    inputs, stores, outs = refs[: stores_at[0]], refs[stores_at[0] : stores_at[1]], refs[stores_at[1] :]
    core = lax.rem(lax.axis_index("tensor"), 2)
    for kind, side, distance, width, source, (target, place) in blocks:
        store = stores[2 * kind + side]
        group = ahead(distance)
        first = core * width if width < WANTED else 0

        def slot(j, carry, store=store, group=group, first=first, source=source, out=outs[target], place=place):
            at, here = panel_of(table_ref, group, first + j, store.shape[0])
            panel = store[at]
            if source is None:
                old = jnp.zeros_like(panel)
            else:
                array, begin, held = source
                there = j - core * held if held < WANTED else j
                old = inputs[array][begin + jnp.clip(there, 0, held - 1)]
                if held < WANTED:
                    old = jnp.where((there >= 0) & (there < held), old, jnp.zeros_like(old))
            out[place + j] = jnp.where(here, panel, old)
            return carry

        lax.fori_loop(0, width, slot, 0, unroll=4)


def joined(table_ref, j, same_ref, cross_ref, store_ref):
    stored = store_ref.shape[0]
    core = lax.rem(lax.axis_index("tensor"), 2)
    group = lax.axis_index("adapter")
    storage = slot_of(table_ref, group, j)
    behind = lax.rem(group - storage // stored + NZ, NZ)
    below = (behind < NZ // 2) | ((behind == NZ // 2) & (j < WANTED // 2))
    own = store_ref[jnp.clip(storage - group * stored, 0, stored - 1)]
    return jnp.where(behind == 0, own, jnp.where(below == (core == 0), same_ref[j], cross_ref[j]))


def join_kernel(table_ref, same_ref, cross_ref, store_ref, out_ref):
    def one(j, carry):
        out_ref[j] = joined(table_ref, j, same_ref, cross_ref, store_ref)
        return carry

    lax.fori_loop(0, out_ref.shape[0], one, 0)


def shrink_kernel(table_ref, here_ref, other_ref, mine_ref, sib_ref, turned_ref, slot_ref, out_ref, panels, parts):
    rank, half = out_ref.shape
    stored = mine_ref.shape[0]
    core = lax.rem(lax.axis_index("tensor"), 2)
    group = lax.axis_index("adapter")
    feats = mine_ref.shape[2]

    def one(j, carry):
        storage = slot_of(table_ref, group, j)
        behind = lax.rem(group - storage // stored + NZ, NZ)
        below = (behind < NZ // 2) | ((behind == NZ // 2) & (j < WANTED // 2))
        at = jnp.clip(storage - group * stored, 0, stored - 1)
        for side, store in enumerate((mine_ref, sib_ref)):
            came = jnp.where(below == (core == 0), here_ref[side * WANTED + j], other_ref[(1 - side) * WANTED + j])
            panels[j, :, side * feats : (side + 1) * feats] = jnp.where(behind == 0, store[at], came)
        return carry

    lax.fori_loop(0, WANTED, one, 0, unroll=2)
    flat = panels[...].reshape(WANTED * rank, 2 * feats)
    parts[...] = jnp.dot(flat, turned_ref[...], preferred_element_type=f32)
    slot = slot_ref[:, pl.ds(pl.multiple_of(core * half, 128), half)]
    total = jnp.zeros((rank, half), f32)
    for j in range(WANTED):
        total = jnp.where(slot == j, parts[j * rank : (j + 1) * rank, :], total)
    out_ref[...] = total


def base_kernel(block_ref, *refs):
    *stacks, mine_ref, sib_ref, out_ref, lefts, weights, sems = refs
    columns = mine_ref.shape[2]
    total = stacks.pop(0) if len(stacks[0].shape) == 3 and stacks[0].shape[2] == columns else None
    pieces = [stack.at[i] for stack in stacks for i in range(stack.shape[0])]

    def fetch(i, side):
        source = (mine_ref, sib_ref)[side].at[block_ref[i]]
        place = weights.at[i, :, side * columns : (side + 1) * columns]
        return pltpu.make_async_copy(source, place, sems.at[i, side])

    def fetch_left(i):
        return pltpu.make_async_copy(pieces[i] if isinstance(i, int) else pieces[0], lefts.at[i], sems.at[i, 2])

    for i in range(len(pieces)):
        fetch_left(i).start()
        for side in range(2):
            fetch(i, side).start()
    out_ref[...] = jnp.zeros_like(out_ref) if total is None else total[...]

    def piece(i, carry):
        fetch_left(i).wait()
        for side in range(2):
            fetch(i, side).wait()
        both = jnp.dot(lefts[i], weights[i], preferred_element_type=f32)
        out_ref[0] += both[:, :columns]
        out_ref[1] += both[:, columns:]
        return carry

    lax.fori_loop(0, len(pieces), piece, 0)


def expand_kernel(panels_ref, scaled_ref, other_ref, slot_ref, here_ref, there_ref, out_ref):
    core = lax.rem(lax.axis_index("tensor"), 2)
    wanted, rank, columns = panels_ref.shape
    half = scaled_ref.shape[1]
    panel = panels_ref[...].reshape(wanted * rank, columns)
    for part in range(2):
        mine = core == part
        scaled = jnp.where(mine, scaled_ref[...], other_ref[...])
        base = jnp.where(mine, here_ref[...], there_ref[...])
        slot = slot_ref[:, part * half : (part + 1) * half]
        delta = jnp.concatenate(
            [jnp.where(slot == j, scaled, jnp.zeros_like(scaled)) for j in range(wanted)], axis=0
        )
        total = base + lax.dot_general(delta, panel, (((0,), (0,)), ((), ())), preferred_element_type=f32)
        out_ref[part * half : (part + 1) * half, :] = total.astype(out_ref.dtype)


def own_kernel(hidden_ref, got_ref, out_ref, turned_ref):
    core = lax.rem(lax.axis_index("tensor"), 2)
    rows, feats = hidden_ref.shape
    half = pl.ds(pl.multiple_of(core * (rows // 2), rows // 2), rows // 2)
    mine, got = hidden_ref[half, :], got_ref[half, :]
    out_ref[:, :feats] = jnp.where(core == 0, mine, got)
    out_ref[:, feats:] = jnp.where(core == 0, got, mine)
    turned_ref[:feats, :] = mine.T
    turned_ref[feats:, :] = got.T


def after(value, *earlier):
    return lax.optimization_barrier((value, *earlier))[0]


def per_device(hidden_rows, query_weight, down_panels, up_panels, store_index, requests, row_slot):
    rows, feats = hidden_rows.shape
    stored, rank, columns = down_panels.shape
    groups, wanted = requests.shape
    t = lax.axis_index("tensor")
    y, x, c = t // 8, (t // 2) % 4, t % 2
    slot_row = row_slot.reshape(1, rows)
    table = jnp.concatenate((requests.reshape(-1), store_index))

    down_sib = to_sibling(down_panels)
    got = to_sibling(hidden_rows)
    sources = (down_panels, up_panels, hidden_rows)
    down_panels, up_panels_here, hidden_rows = kernel_call(
        load_kernel, tuple(jax.ShapeDtypeStruct(v.shape, bf16) for v in sources),
        *[pltpu.with_memory_space_constraint(v, pltpu.HBM) for v in sources],
        specs=[ANY] * 3, scratch=[pltpu.SemaphoreType.DMA((3,))],
    )

    def step(parts, sizes, inputs, *earlier):
        stores = (down_panels, down_sib) + ((up_panels_here, up_sib) if any(part[0] for part in parts) else ())
        inputs = [after(value, *earlier) for value in inputs]
        ends = (len(inputs), len(inputs) + len(stores))
        return kernel_call(
            functools.partial(fill_kernel, parts, ends),
            tuple(jax.ShapeDtypeStruct((size, rank, columns), bf16) for size in sizes),
            after(table, *earlier), *inputs, *stores,
        )

    def blocks(firsts, second):
        out = []
        for first in firsts:
            sy = y + jnp.where(c == 0, second, first)
            sx = x + jnp.where(c == 0, first, second)
            out.append((sy % 4) * 4 + sx % 4)
        return out

    weight_shape = (16, 2 * feats, columns)

    def add_base(total, *parts):
        order = sum([blocks(firsts, second) for _, firsts, second in parts], [])
        stacks = [stack for stack, _, _ in parts]
        operands = ([] if total is None else [total]) + stacks
        return kernel_call(
            base_kernel,
            jax.ShapeDtypeStruct((2, rows // 2, columns), f32),
            jnp.stack(order).astype(i32), *operands,
            pltpu.with_memory_space_constraint(query_weight.reshape(weight_shape), pltpu.HBM),
            weight_sib.reshape(weight_shape),
            specs=[SMEM] + ([] if total is None else [VMEM]) + [ANY] * (len(stacks) + 2), pin=False,
            scratch=[
                pltpu.VMEM((len(order), rows // 2, 2 * feats), bf16),
                pltpu.VMEM((len(order), 2 * feats, 2 * columns), bf16),
                pltpu.SemaphoreType.DMA((len(order), 3)),
            ],
        )

    near_at, rest_at = (0, -1), (1, 2)
    few, all_of = wanted // 2, wanted
    (ring1,) = step(
        [(0, 0, 4, few, None, (0, 0)), (0, 1, 4, few, None, (0, few))], (2 * few,), [], down_sib
    )
    hop1 = along_z(ring1)
    own_piece, turned = kernel_call(
        own_kernel,
        (jax.ShapeDtypeStruct((rows // 2, 2 * feats), bf16), jax.ShapeDtypeStruct((2 * feats, rows // 2), bf16)),
        hidden_rows, after(got, ring1),
    )
    below, above = along_first(own_piece, 1), along_first(own_piece, -1)
    up_sib = to_sibling(after(up_panels, own_piece))
    weight_sib = to_sibling(after(query_weight, own_piece))

    (ring2,) = step(
        [
            (0, 0, 3, all_of, (0, 0, few), (0, 0)), (0, 1, 3, all_of, (0, few, few), (0, all_of)),
            (1, 0, 4, few, None, (0, 2 * all_of)), (1, 1, 4, few, None, (0, 2 * all_of + few)),
        ],
        (3 * all_of,), [hop1], own_piece, up_sib, below, above,
    )
    hop2 = along_z(ring2)
    below, above = after((below, above), ring2)
    near = jnp.stack((own_piece, below))
    near_below, near_above, beyond = along_second(near, 1), along_second(near, -1), along_first(below, 1)

    (ring3,) = step(
        [
            (0, 0, 2, all_of, (0, 0, all_of), (0, 0)), (0, 1, 2, all_of, (0, all_of, all_of), (0, all_of)),
            (1, 0, 3, all_of, (0, 2 * all_of, few), (0, 2 * all_of)),
            (1, 1, 3, all_of, (0, 2 * all_of + few, few), (0, 3 * all_of)),
        ],
        (4 * all_of,), [hop2], near, beyond,
    )
    hop3 = along_z(ring3)
    near_below, near_above, beyond = after((near_below, near_above, beyond), ring3)
    rest = jnp.stack((above, beyond))
    rest_below, rest_above, near_beyond = along_second(rest, 1), along_second(rest, -1), along_second(near_below, 1)
    base = add_base(None, (after(near, rest), near_at, 0), (near_below, near_at, -1), (near_above, near_at, 1))

    ring4, ring4_up = step(
        [
            (0, 0, 1, all_of, (0, 0, all_of), (0, 0)), (0, 1, 1, all_of, (0, all_of, all_of), (0, all_of)),
            (1, 0, 2, all_of, (0, 2 * all_of, all_of), (1, 0)), (1, 1, 2, all_of, (0, 3 * all_of, all_of), (1, all_of)),
        ],
        (2 * all_of, 2 * all_of), [hop3], base,
    )
    hop4, hop4_up = along_z(ring4), along_z(ring4_up)
    rest_below, rest_above = after((rest_below, rest_above), ring4)
    rest_beyond = along_second(rest_above, -1)
    base = add_base(
        base, (rest, rest_at, 0), (rest_below, rest_at, -1), (rest_above, rest_at, 1),
    )

    with jax.named_scope("shrink"):
        hop4 = after(hop4, base)
        part = kernel_call(
            shrink_kernel, jax.ShapeDtypeStruct((rank, rows // 2), f32),
            table, hop4, to_sibling(hop4), down_panels, down_sib, turned, slot_row,
            scratch=[pltpu.VMEM((wanted, rank, 2 * feats), bf16), pltpu.VMEM((wanted * rank, rows // 2), f32)],
        )
    with jax.named_scope("shrink_sum"):
        part = after(part, near_beyond)
        pieces = along_x(part, 1), along_x(part, -1), along_x(part, 2)
    up_to_same, up_to_cross = step(
        [
            (1, 0, 1, all_of, (0, 0, all_of), (0, 0)), (1, 1, 1, all_of, (0, all_of, all_of), (1, 0)),
        ],
        (all_of, all_of), [hop4_up], part,
    )
    up_same, up_cross = along_z(up_to_same), along_z(up_to_cross, 1)
    with jax.named_scope("shrink_sum"):
        pieces = after(pieces, up_to_same, rest_beyond)
        part = part + pieces[0] + pieces[1] + pieces[2]
        pieces = along_y(part, 1), along_y(part, -1), along_y(part, 2)
    base = add_base(after(base, part), (near_beyond, near_at, 2), (rest_beyond, rest_at, 2))
    up_here = kernel_call(
        join_kernel, jax.ShapeDtypeStruct((wanted, rank, columns), bf16), table, after(up_same, base), up_cross, up_panels_here
    )
    with jax.named_scope("shrink_sum"):
        pieces = after(pieces, up_here)
        part = part + pieces[0] + pieces[1] + pieces[2]
        scaled = (part * adapter_scale).astype(bf16)
        scaled_other = to_sibling(scaled)
    with jax.named_scope("base"):
        base_here = base[0]
        base_there = to_sibling(after(base[1], scaled))

    with jax.named_scope("expand"):
        return kernel_call(
            expand_kernel, jax.ShapeDtypeStruct((rows, columns), bf16),
            up_here, scaled, scaled_other, slot_row, base_here, base_there,
        )


def solution(mesh):
    return jax.shard_map(
        per_device,
        mesh=mesh,
        in_specs=(
            P("adapter", "tensor"),
            P(None, "tensor"),
            P("adapter", None, "tensor"),
            P("adapter", None, "tensor"),
            P(),
            P(),
            P("adapter"),
        ),
        out_specs=P("adapter", "tensor"),
        check_vma=False,
    )
```

```python
import functools

import jax
import jax.numpy as jnp
from jax import lax
from jax.experimental import pallas as pl
from jax.experimental.pallas import tpu as pltpu
from jax.sharding import PartitionSpec as P

adapter_scale = 0.5
f32, bf16, i32 = jnp.float32, jnp.bfloat16, jnp.int32
NZ, NY, NX, NC = 8, 4, 4, 2
WANTED = 8
INDEX = NZ * WANTED
SMEM = pl.BlockSpec(memory_space=pltpu.SMEM)
VMEM = pl.BlockSpec(memory_space=pltpu.VMEM)
HBM = pl.BlockSpec(memory_space=pltpu.HBM)
ANY = pl.BlockSpec(memory_space=pl.ANY)


def kernel_call(kernel, out_shape, *operands, scratch=(), specs=None, limit=16 << 20, pin=True):
    specs = specs or [SMEM if v.dtype == i32 and v.size <= 256 else VMEM for v in operands]
    if pin:
        operands = [
            pltpu.with_memory_space_constraint(v, pltpu.VMEM) if spec is VMEM and v.size > 1024 else v
            for v, spec in zip(operands, specs)
        ]
        out_shape = jax.tree.map(lambda leaf: pltpu.VMEM(leaf.shape, leaf.dtype), out_shape)
    return pl.pallas_call(
        kernel,
        out_shape=out_shape,
        in_specs=specs,
        out_specs=jax.tree.map(lambda _: VMEM, out_shape),
        scratch_shapes=list(scratch),
        compiler_params=pltpu.CompilerParams(vmem_limit_bytes=limit),
    )(*operands)


def load_kernel(*refs):
    *sources, sems = refs
    sources, targets = sources[: len(sources) // 2], sources[len(sources) // 2 :]
    loads = [pltpu.make_async_copy(a, b, sems.at[i]) for i, (a, b) in enumerate(zip(sources, targets))]
    for load in loads:
        load.start()
    for load in loads:
        load.wait()


def send(value, to):
    pairs = []
    for z in range(NZ):
        for y in range(NY):
            for x in range(NX):
                for c in range(NC):
                    tz, ty, tx, tc = to(z, y, x, c)
                    here = ((z * NY + y) * NX + x) * NC + c
                    there = ((tz % NZ * NY + ty % NY) * NX + tx % NX) * NC + tc
                    pairs.append((here, there))
    return lax.ppermute(value, ("adapter", "tensor"), pairs)


def to_sibling(value):
    return send(value, lambda z, y, x, c: (z, y, x, 1 - c))


def along_z(value, cross=0):
    return send(value, lambda z, y, x, c: (z + 1 - 2 * c, y, x, c ^ cross))


def along_x(value, step):
    return send(value, lambda z, y, x, c: (z, y, x + step, c))


def along_y(value, step):
    return send(value, lambda z, y, x, c: (z, y + step, x, c))


def along_first(value, step):
    return send(value, lambda z, y, x, c: (z, y + step * c, x + step * (1 - c), c))


def along_second(value, step):
    return send(value, lambda z, y, x, c: (z, y + step * (1 - c), x + step * c, c))


def slot_of(table_ref, group, at):
    return table_ref[INDEX + table_ref[group * WANTED + at]]


def panel_of(table_ref, group, at, stored):
    local = slot_of(table_ref, group, at) - lax.axis_index("adapter") * stored
    return jnp.clip(local, 0, stored - 1), (local >= 0) & (local < stored)


def ahead(distance):
    sign = 1 - 2 * lax.rem(lax.axis_index("tensor"), 2)
    return lax.rem(lax.axis_index("adapter") + sign * distance + NZ, NZ)


def fill_kernel(blocks, stores_at, table_ref, *refs):
    inputs, stores, outs = refs[: stores_at[0]], refs[stores_at[0] : stores_at[1]], refs[stores_at[1] :]
    core = lax.rem(lax.axis_index("tensor"), 2)
    for kind, side, distance, width, source, (target, place) in blocks:
        store = stores[2 * kind + side]
        group = ahead(distance)
        first = core * width if width < WANTED else 0

        def slot(j, carry, store=store, group=group, first=first, source=source, out=outs[target], place=place):
            at, here = panel_of(table_ref, group, first + j, store.shape[0])
            panel = store[at]
            if source is None:
                old = jnp.zeros_like(panel)
            else:
                array, begin, held = source
                there = j - core * held if held < WANTED else j
                old = inputs[array][begin + jnp.clip(there, 0, held - 1)]
                if held < WANTED:
                    old = jnp.where((there >= 0) & (there < held), old, jnp.zeros_like(old))
            out[place + j] = jnp.where(here, panel, old)
            return carry

        lax.fori_loop(0, width, slot, 0, unroll=True)


def joined(table_ref, j, same_ref, cross_ref, store_ref):
    stored = store_ref.shape[0]
    core = lax.rem(lax.axis_index("tensor"), 2)
    group = lax.axis_index("adapter")
    storage = slot_of(table_ref, group, j)
    behind = lax.rem(group - storage // stored + NZ, NZ)
    below = (behind < NZ // 2) | ((behind == NZ // 2) & (j < WANTED // 2))
    own = store_ref[jnp.clip(storage - group * stored, 0, stored - 1)]
    return jnp.where(behind == 0, own, jnp.where(below == (core == 0), same_ref[j], cross_ref[j]))


def join_kernel(table_ref, same_ref, cross_ref, store_ref, out_ref):
    def one(j, carry):
        out_ref[j] = joined(table_ref, j, same_ref, cross_ref, store_ref)
        return carry

    lax.fori_loop(0, out_ref.shape[0], one, 0)


def shrink_kernel(table_ref, here_ref, other_ref, mine_ref, sib_ref, turned_ref, slot_ref, out_ref, panels, parts):
    rank, half = out_ref.shape
    stored = mine_ref.shape[0]
    core = lax.rem(lax.axis_index("tensor"), 2)
    group = lax.axis_index("adapter")
    feats = mine_ref.shape[2]

    def one(j, carry):
        storage = slot_of(table_ref, group, j)
        behind = lax.rem(group - storage // stored + NZ, NZ)
        below = (behind < NZ // 2) | ((behind == NZ // 2) & (j < WANTED // 2))
        at = jnp.clip(storage - group * stored, 0, stored - 1)
        for side, store in enumerate((mine_ref, sib_ref)):
            came = jnp.where(below == (core == 0), here_ref[side * WANTED + j], other_ref[(1 - side) * WANTED + j])
            panels[j, :, side * feats : (side + 1) * feats] = jnp.where(behind == 0, store[at], came)
        return carry

    lax.fori_loop(0, WANTED, one, 0, unroll=True)
    flat = panels[...].reshape(WANTED * rank, 2 * feats)
    parts[...] = jnp.dot(flat, turned_ref[...], preferred_element_type=f32)
    slot = slot_ref[:, pl.ds(pl.multiple_of(core * half, 128), half)]
    total = jnp.zeros((rank, half), f32)
    for j in range(WANTED):
        total = jnp.where(slot == j, parts[j * rank : (j + 1) * rank, :], total)
    out_ref[...] = total


def base_kernel(block_ref, *refs):
    *stacks, mine_ref, sib_ref, out_ref, lefts, weights, sems = refs
    columns = mine_ref.shape[2]
    total = stacks.pop(0) if len(stacks[0].shape) == 3 and stacks[0].shape[2] == columns else None
    pieces = [stack.at[i] for stack in stacks for i in range(stack.shape[0])]

    def fetch(i, side):
        source = (mine_ref, sib_ref)[side].at[block_ref[i]]
        place = weights.at[i, :, side * columns : (side + 1) * columns]
        return pltpu.make_async_copy(source, place, sems.at[i, side])

    def fetch_left(i):
        return pltpu.make_async_copy(pieces[i] if isinstance(i, int) else pieces[0], lefts.at[i], sems.at[i, 2])

    for i in range(len(pieces)):
        fetch_left(i).start()
        for side in range(2):
            fetch(i, side).start()
    out_ref[...] = jnp.zeros_like(out_ref) if total is None else total[...]

    def piece(i, carry):
        fetch_left(i).wait()
        for side in range(2):
            fetch(i, side).wait()
        both = jnp.dot(lefts[i], weights[i], preferred_element_type=f32)
        out_ref[0] += both[:, :columns]
        out_ref[1] += both[:, columns:]
        return carry

    lax.fori_loop(0, len(pieces), piece, 0)


def expand_kernel(panels_ref, scaled_ref, other_ref, slot_ref, here_ref, there_ref, out_ref):
    core = lax.rem(lax.axis_index("tensor"), 2)
    wanted, rank, columns = panels_ref.shape
    half = scaled_ref.shape[1]
    panel = panels_ref[...].reshape(wanted * rank, columns)
    for part in range(2):
        mine = core == part
        scaled = jnp.where(mine, scaled_ref[...], other_ref[...])
        base = jnp.where(mine, here_ref[...], there_ref[...])
        slot = slot_ref[:, part * half : (part + 1) * half]
        delta = jnp.concatenate(
            [jnp.where(slot == j, scaled, jnp.zeros_like(scaled)) for j in range(wanted)], axis=0
        )
        total = base + lax.dot_general(delta, panel, (((0,), (0,)), ((), ())), preferred_element_type=f32)
        out_ref[part * half : (part + 1) * half, :] = total.astype(out_ref.dtype)


def own_kernel(hidden_ref, got_ref, out_ref, turned_ref):
    core = lax.rem(lax.axis_index("tensor"), 2)
    rows, feats = hidden_ref.shape
    half = pl.ds(pl.multiple_of(core * (rows // 2), rows // 2), rows // 2)
    mine, got = hidden_ref[half, :], got_ref[half, :]
    out_ref[:, :feats] = jnp.where(core == 0, mine, got)
    out_ref[:, feats:] = jnp.where(core == 0, got, mine)
    turned_ref[:feats, :] = mine.T
    turned_ref[feats:, :] = got.T


def after(value, *earlier):
    return lax.optimization_barrier((value, *earlier))[0]


def per_device(hidden_rows, query_weight, down_panels, up_panels, store_index, requests, row_slot):
    rows, feats = hidden_rows.shape
    stored, rank, columns = down_panels.shape
    groups, wanted = requests.shape
    t = lax.axis_index("tensor")
    y, x, c = t // 8, (t // 2) % 4, t % 2
    slot_row = row_slot.reshape(1, rows)
    table = jnp.concatenate((requests.reshape(-1), store_index))

    down_sib = to_sibling(down_panels)
    got = to_sibling(hidden_rows)
    sources = (down_panels, up_panels, hidden_rows)
    down_panels, up_panels_here, hidden_rows = kernel_call(
        load_kernel, tuple(jax.ShapeDtypeStruct(v.shape, bf16) for v in sources),
        *[pltpu.with_memory_space_constraint(v, pltpu.HBM) for v in sources],
        specs=[ANY] * 3, scratch=[pltpu.SemaphoreType.DMA((3,))],
    )

    def step(parts, sizes, inputs, *earlier):
        stores = (down_panels, down_sib) + ((up_panels_here, up_sib) if any(part[0] for part in parts) else ())
        inputs = [after(value, *earlier) for value in inputs]
        ends = (len(inputs), len(inputs) + len(stores))
        return kernel_call(
            functools.partial(fill_kernel, parts, ends),
            tuple(jax.ShapeDtypeStruct((size, rank, columns), bf16) for size in sizes),
            after(table, *earlier), *inputs, *stores,
        )

    def blocks(firsts, second):
        out = []
        for first in firsts:
            sy = y + jnp.where(c == 0, second, first)
            sx = x + jnp.where(c == 0, first, second)
            out.append((sy % 4) * 4 + sx % 4)
        return out

    weight_shape = (16, 2 * feats, columns)

    def add_base(total, *parts):
        order = sum([blocks(firsts, second) for _, firsts, second in parts], [])
        stacks = [stack for stack, _, _ in parts]
        operands = ([] if total is None else [total]) + stacks
        return kernel_call(
            base_kernel,
            jax.ShapeDtypeStruct((2, rows // 2, columns), f32),
            jnp.stack(order).astype(i32), *operands,
            pltpu.with_memory_space_constraint(query_weight.reshape(weight_shape), pltpu.HBM),
            weight_sib.reshape(weight_shape),
            specs=[SMEM] + ([] if total is None else [VMEM]) + [ANY] * (len(stacks) + 2), pin=False,
            scratch=[
                pltpu.VMEM((len(order), rows // 2, 2 * feats), bf16),
                pltpu.VMEM((len(order), 2 * feats, 2 * columns), bf16),
                pltpu.SemaphoreType.DMA((len(order), 3)),
            ],
        )

    near_at, rest_at = (0, -1), (1, 2)
    few, all_of = wanted // 2, wanted
    (ring1,) = step(
        [(0, 0, 4, few, None, (0, 0)), (0, 1, 4, few, None, (0, few))], (2 * few,), [], down_sib
    )
    hop1 = along_z(ring1)
    own_piece, turned = kernel_call(
        own_kernel,
        (jax.ShapeDtypeStruct((rows // 2, 2 * feats), bf16), jax.ShapeDtypeStruct((2 * feats, rows // 2), bf16)),
        hidden_rows, after(got, ring1),
    )
    below, above = along_first(own_piece, 1), along_first(own_piece, -1)
    up_sib = to_sibling(after(up_panels, own_piece))
    weight_sib = to_sibling(after(query_weight, own_piece))

    (ring2,) = step(
        [
            (0, 0, 3, all_of, (0, 0, few), (0, 0)), (0, 1, 3, all_of, (0, few, few), (0, all_of)),
            (1, 0, 4, few, None, (0, 2 * all_of)), (1, 1, 4, few, None, (0, 2 * all_of + few)),
        ],
        (3 * all_of,), [hop1], own_piece, up_sib, below, above,
    )
    hop2 = along_z(ring2)
    below, above = after((below, above), ring2)
    near = jnp.stack((own_piece, below))
    near_below, near_above, beyond = along_second(near, 1), along_second(near, -1), along_first(below, 1)

    (ring3,) = step(
        [
            (0, 0, 2, all_of, (0, 0, all_of), (0, 0)), (0, 1, 2, all_of, (0, all_of, all_of), (0, all_of)),
            (1, 0, 3, all_of, (0, 2 * all_of, few), (0, 2 * all_of)),
            (1, 1, 3, all_of, (0, 2 * all_of + few, few), (0, 3 * all_of)),
        ],
        (4 * all_of,), [hop2], near, beyond,
    )
    hop3 = along_z(ring3)
    near_below, near_above, beyond = after((near_below, near_above, beyond), ring3)
    rest = jnp.stack((above, beyond))
    rest_below, rest_above, near_beyond = along_second(rest, 1), along_second(rest, -1), along_second(near_below, 1)
    base = add_base(None, (after(near, rest), near_at, 0), (near_below, near_at, -1), (near_above, near_at, 1))

    ring4, ring4_up = step(
        [
            (0, 0, 1, all_of, (0, 0, all_of), (0, 0)), (0, 1, 1, all_of, (0, all_of, all_of), (0, all_of)),
            (1, 0, 2, all_of, (0, 2 * all_of, all_of), (1, 0)), (1, 1, 2, all_of, (0, 3 * all_of, all_of), (1, all_of)),
        ],
        (2 * all_of, 2 * all_of), [hop3], base,
    )
    hop4, hop4_up = along_z(ring4), along_z(ring4_up)
    rest_below, rest_above = after((rest_below, rest_above), ring4)
    rest_beyond = along_second(rest_above, -1)
    base = add_base(
        base, (rest, rest_at, 0), (rest_below, rest_at, -1), (rest_above, rest_at, 1),
    )

    with jax.named_scope("shrink"):
        hop4 = after(hop4, base)
        part = kernel_call(
            shrink_kernel, jax.ShapeDtypeStruct((rank, rows // 2), f32),
            table, hop4, to_sibling(hop4), down_panels, down_sib, turned, slot_row,
            scratch=[pltpu.VMEM((wanted, rank, 2 * feats), bf16), pltpu.VMEM((wanted * rank, rows // 2), f32)],
        )
    with jax.named_scope("shrink_sum"):
        part = after(part, near_beyond)
        pieces = along_x(part, 1), along_x(part, -1), along_x(part, 2)
    up_to_same, up_to_cross = step(
        [
            (1, 0, 1, all_of, (0, 0, all_of), (0, 0)), (1, 1, 1, all_of, (0, all_of, all_of), (1, 0)),
        ],
        (all_of, all_of), [hop4_up], part,
    )
    up_same, up_cross = along_z(up_to_same), along_z(up_to_cross, 1)
    with jax.named_scope("shrink_sum"):
        pieces = after(pieces, up_to_same, rest_beyond)
        part = part + pieces[0] + pieces[1] + pieces[2]
        pieces = along_y(part, 1), along_y(part, -1), along_y(part, 2)
    base = add_base(after(base, part), (near_beyond, near_at, 2), (rest_beyond, rest_at, 2))
    up_here = kernel_call(
        join_kernel, jax.ShapeDtypeStruct((wanted, rank, columns), bf16), table, after(up_same, base), up_cross, up_panels_here
    )
    with jax.named_scope("shrink_sum"):
        pieces = after(pieces, up_here)
        part = part + pieces[0] + pieces[1] + pieces[2]
        scaled = (part * adapter_scale).astype(bf16)
        scaled_other = to_sibling(scaled)
    with jax.named_scope("base"):
        base_here = base[0]
        base_there = to_sibling(after(base[1], scaled))

    with jax.named_scope("expand"):
        return kernel_call(
            expand_kernel, jax.ShapeDtypeStruct((rows, columns), bf16),
            up_here, scaled, scaled_other, slot_row, base_here, base_there,
        )


def solution(mesh):
    return jax.shard_map(
        per_device,
        mesh=mesh,
        in_specs=(
            P("adapter", "tensor"),
            P(None, "tensor"),
            P("adapter", None, "tensor"),
            P("adapter", None, "tensor"),
            P(),
            P(),
            P("adapter"),
        ),
        out_specs=P("adapter", "tensor"),
        check_vma=False,
    )
```

```python
import functools

import jax
import jax.numpy as jnp
from jax import lax
from jax.experimental import pallas as pl
from jax.experimental.pallas import tpu as pltpu
from jax.sharding import PartitionSpec as P

adapter_scale = 0.5
f32, bf16, i32 = jnp.float32, jnp.bfloat16, jnp.int32
NZ, NY, NX, NC = 8, 4, 4, 2
WANTED = 8
INDEX = NZ * WANTED
SMEM = pl.BlockSpec(memory_space=pltpu.SMEM)
VMEM = pl.BlockSpec(memory_space=pltpu.VMEM)
HBM = pl.BlockSpec(memory_space=pltpu.HBM)
ANY = pl.BlockSpec(memory_space=pl.ANY)


def kernel_call(kernel, out_shape, *operands, scratch=(), specs=None, limit=16 << 20, pin=True):
    specs = specs or [SMEM if v.dtype == i32 and v.size <= 256 else VMEM for v in operands]
    if pin:
        operands = [
            pltpu.with_memory_space_constraint(v, pltpu.VMEM) if spec is VMEM and v.size > 1024 else v
            for v, spec in zip(operands, specs)
        ]
        out_shape = jax.tree.map(lambda leaf: pltpu.VMEM(leaf.shape, leaf.dtype), out_shape)
    return pl.pallas_call(
        kernel,
        out_shape=out_shape,
        in_specs=specs,
        out_specs=jax.tree.map(lambda _: VMEM, out_shape),
        scratch_shapes=list(scratch),
        compiler_params=pltpu.CompilerParams(vmem_limit_bytes=limit),
    )(*operands)


def load_kernel(*refs):
    *sources, sems = refs
    sources, targets = sources[: len(sources) // 2], sources[len(sources) // 2 :]
    loads = [pltpu.make_async_copy(a, b, sems.at[i]) for i, (a, b) in enumerate(zip(sources, targets))]
    for load in loads:
        load.start()
    for load in loads:
        load.wait()


def send(value, to):
    pairs = []
    for z in range(NZ):
        for y in range(NY):
            for x in range(NX):
                for c in range(NC):
                    tz, ty, tx, tc = to(z, y, x, c)
                    here = ((z * NY + y) * NX + x) * NC + c
                    there = ((tz % NZ * NY + ty % NY) * NX + tx % NX) * NC + tc
                    pairs.append((here, there))
    return lax.ppermute(value, ("adapter", "tensor"), pairs)


def to_sibling(value):
    return send(value, lambda z, y, x, c: (z, y, x, 1 - c))


def along_z(value, cross=0):
    return send(value, lambda z, y, x, c: (z + 1 - 2 * c, y, x, c ^ cross))


def along_x(value, step):
    return send(value, lambda z, y, x, c: (z, y, x + step, c))


def along_y(value, step):
    return send(value, lambda z, y, x, c: (z, y + step, x, c))


def along_first(value, step):
    return send(value, lambda z, y, x, c: (z, y + step * c, x + step * (1 - c), c))


def along_second(value, step):
    return send(value, lambda z, y, x, c: (z, y + step * (1 - c), x + step * c, c))


def slot_of(table_ref, group, at):
    return table_ref[INDEX + table_ref[group * WANTED + at]]


def panel_of(table_ref, group, at, stored):
    local = slot_of(table_ref, group, at) - lax.axis_index("adapter") * stored
    return jnp.clip(local, 0, stored - 1), (local >= 0) & (local < stored)


def ahead(distance):
    sign = 1 - 2 * lax.rem(lax.axis_index("tensor"), 2)
    return lax.rem(lax.axis_index("adapter") + sign * distance + NZ, NZ)


def fill_kernel(blocks, stores_at, table_ref, *refs):
    inputs, stores, outs = refs[: stores_at[0]], refs[stores_at[0] : stores_at[1]], refs[stores_at[1] :]
    core = lax.rem(lax.axis_index("tensor"), 2)
    for kind, side, distance, width, source, (target, place) in blocks:
        store = stores[2 * kind + side]
        group = ahead(distance)
        first = core * width if width < WANTED else 0

        def slot(j, carry, store=store, group=group, first=first, source=source, out=outs[target], place=place):
            at, here = panel_of(table_ref, group, first + j, store.shape[0])
            panel = store[at]
            if source is None:
                old = jnp.zeros_like(panel)
            else:
                array, begin, held = source
                there = j - core * held if held < WANTED else j
                old = inputs[array][begin + jnp.clip(there, 0, held - 1)]
                if held < WANTED:
                    old = jnp.where((there >= 0) & (there < held), old, jnp.zeros_like(old))
            out[place + j] = jnp.where(here, panel, old)
            return carry

        lax.fori_loop(0, width, slot, 0, unroll=True)


def joined(table_ref, j, same_ref, cross_ref, store_ref):
    stored = store_ref.shape[0]
    core = lax.rem(lax.axis_index("tensor"), 2)
    group = lax.axis_index("adapter")
    storage = slot_of(table_ref, group, j)
    behind = lax.rem(group - storage // stored + NZ, NZ)
    below = (behind < NZ // 2) | ((behind == NZ // 2) & (j < WANTED // 2))
    own = store_ref[jnp.clip(storage - group * stored, 0, stored - 1)]
    return jnp.where(behind == 0, own, jnp.where(below == (core == 0), same_ref[j], cross_ref[j]))


def join_kernel(table_ref, same_ref, cross_ref, store_ref, out_ref):
    def one(j, carry):
        out_ref[j] = joined(table_ref, j, same_ref, cross_ref, store_ref)
        return carry

    lax.fori_loop(0, out_ref.shape[0], one, 0)


def shrink_kernel(table_ref, here_ref, other_ref, mine_ref, sib_ref, turned_ref, slot_ref, out_ref, panels, parts):
    rank, half = out_ref.shape
    stored = mine_ref.shape[0]
    core = lax.rem(lax.axis_index("tensor"), 2)
    group = lax.axis_index("adapter")
    feats = mine_ref.shape[2]

    def one(j, carry):
        storage = slot_of(table_ref, group, j)
        behind = lax.rem(group - storage // stored + NZ, NZ)
        below = (behind < NZ // 2) | ((behind == NZ // 2) & (j < WANTED // 2))
        at = jnp.clip(storage - group * stored, 0, stored - 1)
        for side, store in enumerate((mine_ref, sib_ref)):
            came = jnp.where(below == (core == 0), here_ref[side * WANTED + j], other_ref[(1 - side) * WANTED + j])
            panels[j, :, side * feats : (side + 1) * feats] = jnp.where(behind == 0, store[at], came)
        return carry

    lax.fori_loop(0, WANTED, one, 0, unroll=True)
    flat = panels[...].reshape(WANTED * rank, 2 * feats)
    parts[...] = jnp.dot(flat, turned_ref[...], preferred_element_type=f32)
    slot = slot_ref[:, pl.ds(pl.multiple_of(core * half, 128), half)]
    total = jnp.zeros((rank, half), f32)
    for j in range(WANTED):
        total = jnp.where(slot == j, parts[j * rank : (j + 1) * rank, :], total)
    out_ref[...] = total


def base_kernel(block_ref, *refs):
    *stacks, mine_ref, sib_ref, out_ref, lefts, weights, sems = refs
    columns = mine_ref.shape[2]
    total = stacks.pop(0) if len(stacks[0].shape) == 3 and stacks[0].shape[2] == columns else None
    pieces = [stack.at[i] for stack in stacks for i in range(stack.shape[0])]

    def fetch(i, side):
        source = (mine_ref, sib_ref)[side].at[block_ref[i]]
        place = weights.at[i, :, side * columns : (side + 1) * columns]
        return pltpu.make_async_copy(source, place, sems.at[i, side])

    def fetch_left(i):
        return pltpu.make_async_copy(pieces[i] if isinstance(i, int) else pieces[0], lefts.at[i], sems.at[i, 2])

    for i in range(len(pieces)):
        fetch_left(i).start()
        for side in range(2):
            fetch(i, side).start()
    out_ref[...] = jnp.zeros_like(out_ref) if total is None else total[...]

    def piece(i, carry):
        fetch_left(i).wait()
        for side in range(2):
            fetch(i, side).wait()
        both = jnp.dot(lefts[i], weights[i], preferred_element_type=f32)
        out_ref[0] += both[:, :columns]
        out_ref[1] += both[:, columns:]
        return carry

    lax.fori_loop(0, len(pieces), piece, 0)


def expand_kernel(panels_ref, scaled_ref, other_ref, slot_ref, here_ref, there_ref, out_ref, halves, sems):
    core = lax.rem(lax.axis_index("tensor"), 2)
    wanted, rank, columns = panels_ref.shape
    half = scaled_ref.shape[1]
    panel = panels_ref[...].reshape(wanted * rank, columns)
    stores = []
    for part in range(2):
        mine = core == part
        scaled = jnp.where(mine, scaled_ref[...], other_ref[...])
        base = jnp.where(mine, here_ref[...], there_ref[...])
        slot = slot_ref[:, part * half : (part + 1) * half]
        delta = jnp.concatenate(
            [jnp.where(slot == j, scaled, jnp.zeros_like(scaled)) for j in range(wanted)], axis=0
        )
        total = base + lax.dot_general(delta, panel, (((0,), (0,)), ((), ())), preferred_element_type=f32)
        halves[part] = total.astype(halves.dtype)
        stores.append(pltpu.make_async_copy(halves.at[part], out_ref.at[pl.ds(part * half, half)], sems.at[part]))
        stores[part].start()
    for store in stores:
        store.wait()


def own_kernel(hidden_ref, got_ref, out_ref, turned_ref):
    core = lax.rem(lax.axis_index("tensor"), 2)
    rows, feats = hidden_ref.shape
    half = pl.ds(pl.multiple_of(core * (rows // 2), rows // 2), rows // 2)
    mine, got = hidden_ref[half, :], got_ref[half, :]
    out_ref[:, :feats] = jnp.where(core == 0, mine, got)
    out_ref[:, feats:] = jnp.where(core == 0, got, mine)
    turned_ref[:feats, :] = mine.T
    turned_ref[feats:, :] = got.T


def after(value, *earlier):
    return lax.optimization_barrier((value, *earlier))[0]


def per_device(hidden_rows, query_weight, down_panels, up_panels, store_index, requests, row_slot):
    rows, feats = hidden_rows.shape
    stored, rank, columns = down_panels.shape
    groups, wanted = requests.shape
    t = lax.axis_index("tensor")
    y, x, c = t // 8, (t // 2) % 4, t % 2
    slot_row = row_slot.reshape(1, rows)
    table = jnp.concatenate((requests.reshape(-1), store_index))

    down_sib = to_sibling(down_panels)
    got = to_sibling(hidden_rows)
    sources = (down_panels, up_panels, hidden_rows)
    down_panels, up_panels_here, hidden_rows = kernel_call(
        load_kernel, tuple(jax.ShapeDtypeStruct(v.shape, bf16) for v in sources),
        *[pltpu.with_memory_space_constraint(v, pltpu.HBM) for v in sources],
        specs=[ANY] * 3, scratch=[pltpu.SemaphoreType.DMA((3,))],
    )

    def step(parts, sizes, inputs, *earlier):
        stores = (down_panels, down_sib) + ((up_panels_here, up_sib) if any(part[0] for part in parts) else ())
        inputs = [after(value, *earlier) for value in inputs]
        ends = (len(inputs), len(inputs) + len(stores))
        return kernel_call(
            functools.partial(fill_kernel, parts, ends),
            tuple(jax.ShapeDtypeStruct((size, rank, columns), bf16) for size in sizes),
            after(table, *earlier), *inputs, *stores,
        )

    def blocks(firsts, second):
        out = []
        for first in firsts:
            sy = y + jnp.where(c == 0, second, first)
            sx = x + jnp.where(c == 0, first, second)
            out.append((sy % 4) * 4 + sx % 4)
        return out

    weight_shape = (16, 2 * feats, columns)

    def add_base(total, *parts):
        order = sum([blocks(firsts, second) for _, firsts, second in parts], [])
        stacks = [stack for stack, _, _ in parts]
        operands = ([] if total is None else [total]) + stacks
        return kernel_call(
            base_kernel,
            jax.ShapeDtypeStruct((2, rows // 2, columns), f32),
            jnp.stack(order).astype(i32), *operands,
            pltpu.with_memory_space_constraint(query_weight.reshape(weight_shape), pltpu.HBM),
            weight_sib.reshape(weight_shape),
            specs=[SMEM] + ([] if total is None else [VMEM]) + [ANY] * (len(stacks) + 2), pin=False,
            scratch=[
                pltpu.VMEM((len(order), rows // 2, 2 * feats), bf16),
                pltpu.VMEM((len(order), 2 * feats, 2 * columns), bf16),
                pltpu.SemaphoreType.DMA((len(order), 3)),
            ],
        )

    near_at, rest_at = (0, -1), (1, 2)
    few, all_of = wanted // 2, wanted
    (ring1,) = step(
        [(0, 0, 4, few, None, (0, 0)), (0, 1, 4, few, None, (0, few))], (2 * few,), [], down_sib
    )
    hop1 = along_z(ring1)
    own_piece, turned = kernel_call(
        own_kernel,
        (jax.ShapeDtypeStruct((rows // 2, 2 * feats), bf16), jax.ShapeDtypeStruct((2 * feats, rows // 2), bf16)),
        hidden_rows, after(got, ring1),
    )
    below, above = along_first(own_piece, 1), along_first(own_piece, -1)
    up_sib = to_sibling(after(up_panels, own_piece))
    weight_sib = to_sibling(after(query_weight, own_piece))

    (ring2,) = step(
        [
            (0, 0, 3, all_of, (0, 0, few), (0, 0)), (0, 1, 3, all_of, (0, few, few), (0, all_of)),
            (1, 0, 4, few, None, (0, 2 * all_of)), (1, 1, 4, few, None, (0, 2 * all_of + few)),
        ],
        (3 * all_of,), [hop1], own_piece, up_sib, below, above,
    )
    hop2 = along_z(ring2)
    below, above = after((below, above), ring2)
    near = jnp.stack((own_piece, below))
    near_below, near_above, beyond = along_second(near, 1), along_second(near, -1), along_first(below, 1)

    (ring3,) = step(
        [
            (0, 0, 2, all_of, (0, 0, all_of), (0, 0)), (0, 1, 2, all_of, (0, all_of, all_of), (0, all_of)),
            (1, 0, 3, all_of, (0, 2 * all_of, few), (0, 2 * all_of)),
            (1, 1, 3, all_of, (0, 2 * all_of + few, few), (0, 3 * all_of)),
        ],
        (4 * all_of,), [hop2], near, beyond,
    )
    hop3 = along_z(ring3)
    near_below, near_above, beyond = after((near_below, near_above, beyond), ring3)
    rest = jnp.stack((above, beyond))
    rest_below, rest_above, near_beyond = along_second(rest, 1), along_second(rest, -1), along_second(near_below, 1)
    base = add_base(None, (after(near, rest), near_at, 0), (near_below, near_at, -1), (near_above, near_at, 1))

    ring4, ring4_up = step(
        [
            (0, 0, 1, all_of, (0, 0, all_of), (0, 0)), (0, 1, 1, all_of, (0, all_of, all_of), (0, all_of)),
            (1, 0, 2, all_of, (0, 2 * all_of, all_of), (1, 0)), (1, 1, 2, all_of, (0, 3 * all_of, all_of), (1, all_of)),
        ],
        (2 * all_of, 2 * all_of), [hop3], base,
    )
    hop4, hop4_up = along_z(ring4), along_z(ring4_up)
    rest_below, rest_above = after((rest_below, rest_above), ring4)
    rest_beyond = along_second(rest_above, -1)
    base = add_base(
        base, (rest, rest_at, 0), (rest_below, rest_at, -1), (rest_above, rest_at, 1),
    )

    with jax.named_scope("shrink"):
        hop4 = after(hop4, base)
        part = kernel_call(
            shrink_kernel, jax.ShapeDtypeStruct((rank, rows // 2), f32),
            table, hop4, to_sibling(hop4), down_panels, down_sib, turned, slot_row,
            scratch=[pltpu.VMEM((wanted, rank, 2 * feats), bf16), pltpu.VMEM((wanted * rank, rows // 2), f32)],
        )
    with jax.named_scope("shrink_sum"):
        part = after(part, near_beyond)
        pieces = along_x(part, 1), along_x(part, -1), along_x(part, 2)
    up_to_same, up_to_cross = step(
        [
            (1, 0, 1, all_of, (0, 0, all_of), (0, 0)), (1, 1, 1, all_of, (0, all_of, all_of), (1, 0)),
        ],
        (all_of, all_of), [hop4_up], part,
    )
    up_same, up_cross = along_z(up_to_same), along_z(up_to_cross, 1)
    with jax.named_scope("shrink_sum"):
        pieces = after(pieces, up_to_same, rest_beyond)
        part = part + pieces[0] + pieces[1] + pieces[2]
        pieces = along_y(part, 1), along_y(part, -1), along_y(part, 2)
    base = add_base(after(base, part), (near_beyond, near_at, 2), (rest_beyond, rest_at, 2))
    up_here = kernel_call(
        join_kernel, jax.ShapeDtypeStruct((wanted, rank, columns), bf16), table, after(up_same, base), up_cross, up_panels_here
    )
    with jax.named_scope("shrink_sum"):
        pieces = after(pieces, up_here)
        part = part + pieces[0] + pieces[1] + pieces[2]
        scaled = (part * adapter_scale).astype(bf16)
        scaled_other = to_sibling(scaled)
    with jax.named_scope("base"):
        base_here = base[0]
        base_there = to_sibling(after(base[1], scaled))

    with jax.named_scope("expand"):
        inputs = up_here, scaled, scaled_other, slot_row, base_here, base_there
        return pl.pallas_call(
            expand_kernel,
            out_shape=jax.ShapeDtypeStruct((rows, columns), bf16),
            in_specs=[VMEM] * len(inputs),
            out_specs=ANY,
            scratch_shapes=[pltpu.VMEM((2, rows // 2, columns), bf16), pltpu.SemaphoreType.DMA((2,))],
            compiler_params=pltpu.CompilerParams(vmem_limit_bytes=16 << 20),
        )(*inputs)


def solution(mesh):
    return jax.shard_map(
        per_device,
        mesh=mesh,
        in_specs=(
            P("adapter", "tensor"),
            P(None, "tensor"),
            P("adapter", None, "tensor"),
            P("adapter", None, "tensor"),
            P(),
            P(),
            P("adapter"),
        ),
        out_specs=P("adapter", "tensor"),
        check_vma=False,
    )
```
